768 devices in a mesh: dom: 32 (over x, y), col: 24 (over z, core).
Axes of the slice: x: 4, y: 8, z: 12, core: 2. Of those that a mesh axis runs over, the one named last changes fastest.
Arguments:
- a_tiles: bfloat16 [64, 96, 12, 128, 128], P('dom', 'col'), may hold values from -6 to 6
- p_tiles: bfloat16 [64, 96, 128, 128], P('dom', 'col'), may hold values from -0.1875 to 0.1875
- a_cols: int32 [64, 96, 12], P('dom', 'col'), may hold values from -1 to 6143, as said below
- slot_map: int32 [64, 96, 12], P('dom', 'col'), may hold values from 0 to 3
- aggregate: int32 [64, 96], P('dom', 'col'), may hold values from 0 to 767, as said below
Outputs:
- coarse_tiles: float32 [32, 24, 4, 128, 128], P('dom', 'col')
The draws below stay inside these ranges and needn't reach their ends.
Inputs may be any that keep to these rules, and one draw needn't show every extreme that they name: `a_cols`: slot 0 of fine tile (x, y) names the tile itself; the other slots name distinct tiles (x', y') with |x' - x| <= 2 and |y' - y| <= 2 inside the grid, or hold -1. `aggregate`: for fine tile (x, y) the coarse tile a * 24 + b has a = x // 2 and b within one of y // 4.
All inputs are finite; a program needn't handle non-finite values.
Results may differ from the reference program's by a relative error of at most 0.0029.
Values may be sent and summed in bfloat16 or wider, within the bound.
A program may use at most 32 MiB of HBM per device.

```python
import jax
import jax.numpy as jnp
import numpy as np
from jax import lax

TILE = 128
COARSE = 128
SLOTS = 12
CSLOTS = 4
FX_DEV = 2
FY_DEV = 4
FX = 64
FY = 96
N_DOM = 32
N_COL = 24


def draw_a_cols(key, part):
    key = jax.random.fold_in(key, 11)
    key_order, key_keep = jax.random.split(key)
    shifts = [(dx, dy) for dx in range(-2, 3) for dy in range(-2, 3) if (dx, dy) != (0, 0)]
    table_x = jnp.asarray(np.array([s[0] for s in shifts], np.int32))
    table_y = jnp.asarray(np.array([s[1] for s in shifts], np.int32))
    scores = jax.random.randint(key_order, (FX, FY, 24), 0, 1 << 20) * 32 + jnp.arange(24, dtype=jnp.int32)
    chosen = jnp.argsort(scores, axis=-1, stable=True)[:, :, :SLOTS - 1]
    grid_x = jnp.arange(FX, dtype=jnp.int32)[:, None, None]
    grid_y = jnp.arange(FY, dtype=jnp.int32)[None, :, None]
    near_x = grid_x + table_x[chosen]
    near_y = grid_y + table_y[chosen]
    inside = (near_x >= 0) & (near_x < FX) & (near_y >= 0) & (near_y < FY)
    keeper = jax.random.randint(key_keep, (FX, FY, SLOTS - 1), 0, 4) > 0
    others = jnp.where(inside & keeper, near_x * FY + near_y, -1)
    itself = jnp.broadcast_to(grid_x * FY + grid_y, (FX, FY, 1))
    return jnp.concatenate([itself, others], axis=-1).astype(jnp.int32)


def draw_aggregate(key, part):
    key = jax.random.fold_in(key, 23)
    col_count = FY // FY_DEV
    grid_x = jnp.arange(FX, dtype=jnp.int32)[:, None]
    grid_y = jnp.arange(FY, dtype=jnp.int32)[None, :]
    block_x = grid_x // FX_DEV
    block_y = grid_y // FY_DEV
    within = grid_y % FY_DEV
    moving = jax.random.randint(key, (FX, FY), 0, 2)
    offset = jnp.where(within == 0, -moving, jnp.where(within == FY_DEV - 1, moving, 0))
    target = jnp.clip(block_y + offset, 0, col_count - 1)
    return (block_x * col_count + target).astype(jnp.int32)


def plant(values, own_key, least, top_value):
    dims = values.shape
    index_at = [jax.random.randint(jax.random.fold_in(own_key, axis), (), 0, dims[axis]) for axis in range(len(dims))]
    values = values.at[tuple(index_at)].set(least)
    longest = dims.index(max(dims))
    index_at[longest] = (index_at[longest] + 1) % dims[longest]
    return values.at[tuple(index_at)].set(top_value)


def block_levels(own_key, extent, pieces, smallest, top_value):
    gain, own = 1.0, jax.random.fold_in(own_key, 6)
    for position, parts in pieces:
        heights = jnp.exp(jax.random.uniform(jax.random.fold_in(own, position), (parts,), jnp.float32, smallest / len(pieces), top_value / len(pieces)))
        gain = gain * jnp.repeat(heights, extent[position] // parts).reshape([-1 if axis == position else 1 for axis in range(len(extent))])
    return gain


def bell_draw(rng, shape, spread, most, shards=(), kind=jnp.bfloat16):
    values = jax.random.normal(rng, shape, jnp.float32) * spread
    if len(shards) > 0:
        values = block_levels(rng, shape, shards, -0.22, 0.18) * values
    return jnp.clip(values, min=-most, max=most).astype(kind)


def setup_inputs(seed: int = 0) -> dict:
    streams_of = jax.random.split(jax.random.key(seed), 6)
    return {
        "a_tiles": bell_draw(streams_of[0], (FX, FY, SLOTS, TILE, TILE), 1.0, 6.0, ((0, 32), (1, 24))),
        "p_tiles": bell_draw(streams_of[1], (FX, FY, TILE, COARSE), (8 * TILE) ** -0.5, 0.1875, ((0, 32), (1, 24))),
        "a_cols": draw_a_cols(jax.random.fold_in(streams_of[5], 71), 0),
        "slot_map": plant(jax.random.randint(streams_of[3], (FX, FY, SLOTS), 0, CSLOTS), jax.random.fold_in(streams_of[3], 1), 0, CSLOTS - 1).astype(jnp.int32),
        "aggregate": draw_aggregate(jax.random.fold_in(streams_of[5], 71), 0),
    }


def reference(a_tiles, p_tiles, a_cols, slot_map, aggregate):
    flat_p = p_tiles.reshape(FX * FY, TILE, COARSE)
    total = N_DOM * N_COL * CSLOTS

    def one_row(carry, items):
        a_row, p_row, col_row, slot_row, agg_row = items
        is_live = col_row >= 0
        index_safe = jnp.where(is_live, col_row, 0).astype(jnp.int32)
        ghosts = flat_p[index_safe]
        product = jnp.einsum('ykab,ykbc->ykac', a_row.astype(jnp.float32), ghosts.astype(jnp.float32)).astype(jnp.bfloat16)
        terms = jnp.einsum('yba,ykbc->ykac', p_row.astype(jnp.float32), product.astype(jnp.float32))
        terms = jnp.where(is_live[:, :, None, None], terms, jnp.zeros_like(terms))
        target = (agg_row[:, None] * CSLOTS + slot_row).astype(jnp.int32)
        carry = carry.at[target.reshape(-1)].add(terms.reshape(-1, COARSE, COARSE))
        return carry, None

    start = jnp.zeros((total, COARSE, COARSE), jnp.float32)
    result, unused = lax.scan(one_row, start, (a_tiles, p_tiles, a_cols, slot_map, aggregate))
    return result.reshape(N_DOM, N_COL, CSLOTS, COARSE, COARSE)
```

```python
import functools

import jax
import jax.numpy as jnp
from jax import lax
from jax.experimental import pallas as pl
from jax.experimental.pallas import tpu as pltpu
from jax.sharding import PartitionSpec as P

CSLOTS = 4
SIDES = 3
PAIRS = 8
MESH = pl.DeviceIdType.MESH
F32 = jnp.float32
BF16 = jnp.bfloat16


def dot(left, right):
    return lax.dot_general(left, right, (((1,), (0,)), ((), ())), preferred_element_type=F32)


def split(value):
    high = value.astype(BF16)
    return high, (value - high.astype(F32)).astype(BF16)


def kernel(
    n_dom, n_col, a_cols, slot_map, aggregate, a_hbm, p_hbm, out,
    a_tiles, halo, p_turned, sums, totals, away, arrived,
    pick_a, pick_g, ends, order, side_ends,
    local_sem, row_send, row_recv, col_send, col_recv, away_send, away_recv,
):
    rows_x, rows_y, slots = a_cols.shape
    tiles = rows_x * rows_y
    tile = p_hbm.shape[-1]
    dom, col = lax.axis_index("dom"), lax.axis_index("col")
    core = lax.rem(col, 2)
    up, down = lax.rem(dom + 1, n_dom), lax.rem(dom + n_dom - 1, n_dom)
    right, left = lax.rem(col + 1, n_col), lax.rem(col + n_col - 1, n_col)
    outer, inner = jnp.where(core == 0, left, right), jnp.where(core == 0, right, left)
    edge = (2 * core, 2 - 2 * core)
    landing = (6 - 6 * core, 6 * core)

    own_p = pltpu.make_async_copy(p_hbm, halo.at[pl.ds(2, 2), pl.ds(2, 4)], local_sem.at[0])
    own_p.start()
    own_a = pltpu.make_async_copy(a_hbm, a_tiles, local_sem.at[1])
    own_a.start()

    barrier = pltpu.get_barrier_semaphore()
    for target in ((up, col), (down, col), (dom, right), (dom, left)):
        pl.semaphore_signal(barrier, inc=1, device_id=target, device_id_type=MESH)
    pl.semaphore_wait(barrier, 4)

    def along_dom(part, way):
        columns = edge[part]
        index = part * 2 + way
        return pltpu.make_async_remote_copy(
            src_ref=p_hbm.at[:, pl.ds(columns, 2)],
            dst_ref=halo.at[pl.ds(4 * way, 2), pl.ds(2 + columns, 2)],
            send_sem=row_send.at[index],
            recv_sem=row_recv.at[index],
            device_id=((up, down)[way], col),
            device_id_type=MESH,
        )

    def along_col(part, piece):
        columns = edge[part]
        index = part * 3 + piece
        rows = pl.ds(2 * piece, 2)
        source = p_hbm.at[:, pl.ds(columns, 2)] if piece == 1 else halo.at[rows, pl.ds(2 + columns, 2)]
        return pltpu.make_async_remote_copy(
            src_ref=source,
            dst_ref=halo.at[rows, pl.ds(landing[part], 2)],
            send_sem=col_send.at[index],
            recv_sem=col_recv.at[index],
            device_id=(dom, (outer, inner)[part]),
            device_id_type=MESH,
        )

    by_row = [[along_dom(part, way) for way in range(2)] for part in range(2)]
    by_col = [[along_col(part, piece) for piece in range(3)] for part in range(2)]
    by_row[0][0].start()
    by_row[0][1].start()
    by_col[0][1].start()
    by_row[1][0].start()
    by_row[1][1].start()
    by_col[1][1].start()

    halo[6, 0] = jnp.zeros((tile, tile), BF16)
    width_y = rows_y * n_col
    origin = (dom * rows_x - 2) * width_y + col * rows_y - 2
    inverse = -(-65536 // width_y)

    def tabulate(t, carry):
        x, y = t // rows_y, lax.rem(t, rows_y)
        near, groups = [], []
        for k in range(slots):
            where = a_cols[x, y, k]
            offset = where - origin
            near.append(jnp.clip(offset - (width_y - 8) * ((offset * inverse) >> 16), 0, 47))
            groups.append(jnp.where(where >= 0, slot_map[x, y, k], CSLOTS))
        begin = jnp.int32(0)
        places = [jnp.int32(-1)] * slots
        ends[t * (CSLOTS + 1)] = 0
        for j in range(CSLOTS):
            count = begin
            for k in range(slots):
                member = groups[k] == j
                places[k] = jnp.where(member, count, places[k])
                count = count + member.astype(jnp.int32)
            begin = (count + 1) & -2
            ends[t * (CSLOTS + 1) + j + 1] = begin >> 1
        for place in range(2 * PAIRS):
            slot, tile_g = jnp.int32(0), jnp.int32(48)
            for k in range(slots):
                here = places[k] == place
                slot = jnp.where(here, k, slot)
                tile_g = jnp.where(here, near[k], tile_g)
            pick_a[t * 2 * PAIRS + place] = t * slots + slot
            pick_g[t * 2 * PAIRS + place] = tile_g
        return carry

    lax.fori_loop(0, tiles, tabulate, 0)

    sides = [
        lax.rem(aggregate[t // rows_y, t % rows_y], n_col) - col + 1 for t in range(tiles)
    ]
    count = jnp.int32(0)
    places = [jnp.int32(0)] * tiles
    side_ends[0] = 0
    for side in range(SIDES):
        for t in range(tiles):
            member = sides[t] == side
            places[t] = jnp.where(member, count, places[t])
            count = count + member.astype(jnp.int32)
        side_ends[side + 1] = count
    for place in range(tiles):
        chosen = jnp.int32(0)
        for t in range(tiles):
            chosen = jnp.where(places[t] == place, t, chosen)
        order[place] = chosen

    own_p.wait()
    for t in range(tiles):
        turned = halo[2 + t // rows_y, 2 + t % rows_y].T
        p_turned[t] = jnp.concatenate([turned, turned], axis=1)

    for part in range(2):
        for way in range(2):
            by_row[part][way].wait_recv()
            by_col[part][2 * way].start()
    own_a.wait()
    for part in range(2):
        for piece in (1, 0, 2):
            by_col[part][piece].wait_recv()

    sums[0] = jnp.zeros((tile, tile), F32)
    totals[0] = jnp.zeros(totals.shape[1:], F32)

    def one_tile(place, carry):
        t = order[place]
        total = None
        for pair in range(PAIRS):
            first = t * 2 * PAIRS + 2 * pair
            lefts, rights = [], []
            for member in range(2):
                lefts.append(a_tiles[pick_a[first + member]])
                g = pick_g[first + member]
                rights.append(halo[g >> 3, g & 7])
            term = dot(jnp.concatenate(lefts, axis=1), jnp.concatenate(rights, axis=0))
            total = term if total is None else total + term
            sums[pair + 1] = total
        highs, lows = [], []
        for j in range(CSLOTS):
            base = t * (CSLOTS + 1) + j
            high, low = split(sums[ends[base + 1]] - sums[ends[base]])
            highs.append(high)
            lows.append(low)
        stacked = jnp.concatenate(
            [jnp.concatenate(highs, axis=1), jnp.concatenate(lows, axis=1)], axis=0
        )
        totals[place + 1] = totals[place] + dot(p_turned[t], stacked)
        return carry

    lax.fori_loop(0, tiles, one_tile, 0)

    def leaving(way):
        return pltpu.make_async_remote_copy(
            src_ref=away.at[way],
            dst_ref=arrived.at[way],
            send_sem=away_send.at[way],
            recv_sem=away_recv.at[way],
            device_id=(dom, (left, right)[way]),
            device_id_type=MESH,
        )

    leave = [leaving(way) for way in range(2)]
    for way in range(2):
        side = 2 * way
        away[way] = (totals[side_ends[side + 1]] - totals[side_ends[side]]).astype(BF16)
        leave[way].start()
    here = totals[side_ends[2]] - totals[side_ends[1]]
    for way in range(2):
        leave[way].wait_recv()
    result = here + arrived[0].astype(F32) + arrived[1].astype(F32)
    for j in range(CSLOTS):
        out[0, 0, j] = result[:, j * tile:(j + 1) * tile]

    for part in range(2):
        for way in range(2):
            by_row[part][way].wait_send()
        for piece in range(3):
            by_col[part][piece].wait_send()
    for way in range(2):
        leave[way].wait_send()


def body(n_dom, n_col, a_tiles, p_tiles, a_cols, slot_map, aggregate):
    rows_x, rows_y, slots, tile, _ = a_tiles.shape
    tiles = rows_x * rows_y
    wide = CSLOTS * tile
    any_space = pl.BlockSpec(memory_space=pl.ANY)
    scalars = pl.BlockSpec(memory_space=pltpu.SMEM)
    return pl.pallas_call(
        functools.partial(kernel, n_dom, n_col),
        out_shape=jax.ShapeDtypeStruct((1, 1, CSLOTS, tile, tile), F32),
        in_specs=[scalars] * 3 + [any_space] * 2,
        out_specs=pl.BlockSpec(memory_space=pltpu.VMEM),
        scratch_shapes=[
            pltpu.VMEM((tiles * slots, tile, tile), BF16),
            pltpu.VMEM((rows_x + 5, rows_y + 4, tile, tile), BF16),
            pltpu.VMEM((tiles, tile, 2 * tile), BF16),
            pltpu.VMEM((PAIRS + 1, tile, tile), F32),
            pltpu.VMEM((tiles + 1, tile, wide), F32),
            pltpu.VMEM((2, tile, wide), BF16),
            pltpu.VMEM((2, tile, wide), BF16),
            pltpu.SMEM((tiles * 2 * PAIRS,), jnp.int32),
            pltpu.SMEM((tiles * 2 * PAIRS,), jnp.int32),
            pltpu.SMEM((tiles * (CSLOTS + 1),), jnp.int32),
            pltpu.SMEM((tiles,), jnp.int32),
            pltpu.SMEM((SIDES + 1,), jnp.int32),
            pltpu.SemaphoreType.DMA((2,)),
            pltpu.SemaphoreType.DMA((4,)),
            pltpu.SemaphoreType.DMA((4,)),
            pltpu.SemaphoreType.DMA((6,)),
            pltpu.SemaphoreType.DMA((6,)),
            pltpu.SemaphoreType.DMA((2,)),
            pltpu.SemaphoreType.DMA((2,)),
        ],
        compiler_params=pltpu.CompilerParams(
            collective_id=0, has_side_effects=True, vmem_limit_bytes=56 * 2**20
        ),
    )(a_cols, slot_map, aggregate, a_tiles.reshape(tiles * slots, tile, tile), p_tiles)


def solution(mesh):
    in_specs = (
        P("dom", "col", None, None, None),
        P("dom", "col", None, None),
        P("dom", "col", None),
        P("dom", "col", None),
        P("dom", "col"),
    )
    out_specs = P("dom", "col", None, None, None)
    call = functools.partial(body, mesh.shape["dom"], mesh.shape["col"])
    return jax.shard_map(call, mesh=mesh, in_specs=in_specs, out_specs=out_specs, check_vma=False)
```

```python
import functools

import jax
import jax.numpy as jnp
from jax import lax
from jax.experimental import pallas as pl
from jax.experimental.pallas import tpu as pltpu
from jax.sharding import PartitionSpec as P

CSLOTS = 4
SIDES = 3
ROWS = 6
GROUPS = ((1, 2, 5, 6), (0, 3, 4, 7))
MESH = pl.DeviceIdType.MESH
F32 = jnp.float32
BF16 = jnp.bfloat16


def dot(left, right):
    return lax.dot_general(left, right, (((1,), (0,)), ((), ())), preferred_element_type=F32)


def split(value):
    high = value.astype(BF16)
    return high, (value - high.astype(F32)).astype(BF16)


def kernel(
    n_dom, n_col, a_cols_hbm, slot_map_hbm, aggregate_hbm, a_hbm, p_hbm, here, arrived,
    a_tiles, near, wide, p_turned, *scratch,
):
    sums, totals = scratch[:8], scratch[8:10]
    (
        a_cols, slot_map, aggregate, away, pick_a, pick_g, ends, order, side_ends,
        own_sem, small_sem, row_send, row_recv, col_send, col_recv, away_send, away_recv,
    ) = scratch[10:]
    rows_x, rows_y, slots = a_cols.shape
    tiles = rows_x * rows_y
    tile = p_hbm.shape[-1]
    dom, col = lax.axis_index("dom"), lax.axis_index("col")
    core = lax.rem(col, 2)
    up, down = lax.rem(dom + 1, n_dom), lax.rem(dom + n_dom - 1, n_dom)
    right, left = lax.rem(col + 1, n_col), lax.rem(col + n_col - 1, n_col)
    outer, inner = jnp.where(core == 0, left, right), jnp.where(core == 0, right, left)
    columns = (3 * core, 1 + core, 3 - 3 * core, 2 - core)
    landing = (5 - 5 * core, 7 - 7 * core, 5 * core, 7 * core)

    own_p = [
        pltpu.make_async_copy(p_hbm.at[:, y], near.at[pl.ds((y + 1) * ROWS + 2, 2)], own_sem.at[y])
        for y in range(rows_y)
    ]
    own_a = pltpu.make_async_copy(a_hbm, a_tiles, own_sem.at[4])
    widen = pltpu.make_async_copy(near, wide.at[pl.ds(ROWS, 6 * ROWS)], own_sem.at[5])
    for copy in own_p:
        copy.start()
    own_a.start()
    small = [
        pltpu.make_async_copy(source, target, small_sem.at[i])
        for i, (source, target) in enumerate(
            ((a_cols_hbm, a_cols), (slot_map_hbm, slot_map), (aggregate_hbm, aggregate))
        )
    ]
    for copy in small:
        copy.start()

    barrier = pltpu.get_barrier_semaphore()
    for target in ((up, col), (down, col), (dom, right), (dom, left)):
        pl.semaphore_signal(barrier, inc=1, device_id=target, device_id_type=MESH)
    pl.semaphore_wait(barrier, 4)

    def along_dom(part, way):
        index = part * 2 + way
        return pltpu.make_async_remote_copy(
            src_ref=p_hbm.at[:, columns[part]],
            dst_ref=near.at[pl.ds((columns[part] + 1) * ROWS + 4 * way, 2)],
            send_sem=row_send.at[index],
            recv_sem=row_recv.at[index],
            device_id=((up, down)[way], col),
            device_id_type=MESH,
        )

    def along_col(part, piece):
        index = part * 3 + piece
        if piece == 1:
            source = p_hbm.at[:, columns[part]]
        else:
            source = near.at[pl.ds((columns[part] + 1) * ROWS + 2 * piece, 2)]
        target = near if part % 2 == 0 else wide
        return pltpu.make_async_remote_copy(
            src_ref=source,
            dst_ref=target.at[pl.ds(landing[part] * ROWS + 2 * piece, 2)],
            send_sem=col_send.at[index],
            recv_sem=col_recv.at[index],
            device_id=(dom, (outer, outer, inner, inner)[part]),
            device_id_type=MESH,
        )

    by_row = [[along_dom(part, way) for way in range(2)] for part in range(4)]
    by_col = [[along_col(part, piece) for piece in range(3)] for part in range(4)]
    for part in range(4):
        by_row[part][0].start()
        by_row[part][1].start()
        by_col[part][1].start()

    for copy in small:
        copy.wait()

    width_y = rows_y * n_col
    origin = (dom * rows_x - 2) * width_y + col * rows_y - 2
    inverse = -(-65536 // width_y)

    def tabulate(t, first_column, most):
        x, y = t // rows_y, t % rows_y
        spots, groups = [], []
        for k in range(slots):
            where = a_cols[x, y, k]
            offset = where - origin
            near_x = (offset * inverse) >> 16
            spot = (offset - near_x * width_y - first_column) * ROWS + near_x
            spots.append(jnp.clip(spot, 0, most))
            groups.append(jnp.where(where >= 0, slot_map[x, y, k], CSLOTS))
        count = jnp.int32(0)
        places = [jnp.int32(-1)] * slots
        ends[t * (CSLOTS + 1)] = 0
        for j in range(CSLOTS):
            for k in range(slots):
                member = groups[k] == j
                places[k] = jnp.where(member, count, places[k])
                count = count + member.astype(jnp.int32)
            ends[t * (CSLOTS + 1) + j + 1] = count
        for place in range(slots):
            slot, spot = jnp.int32(0), jnp.int32(0)
            for k in range(slots):
                chosen = places[k] == place
                slot = jnp.where(chosen, k, slot)
                spot = jnp.where(chosen, spots[k], spot)
            pick_a[t * slots + place] = t * slots + slot
            pick_g[t * slots + place] = spot

    def put_in_order(group):
        members = GROUPS[group]
        sides = [
            lax.rem(aggregate[t // rows_y, t % rows_y], n_col) - col + 1 for t in members
        ]
        count = jnp.int32(0)
        places = [jnp.int32(0)] * len(members)
        side_ends[group * (SIDES + 1)] = 0
        for side in range(SIDES):
            for i in range(len(members)):
                member = sides[i] == side
                places[i] = jnp.where(member, count, places[i])
                count = count + member.astype(jnp.int32)
            side_ends[group * (SIDES + 1) + side + 1] = count
        for place in range(len(members)):
            chosen = jnp.int32(members[0])
            for i, t in enumerate(members):
                chosen = jnp.where(places[i] == place, t, chosen)
            order[group * len(members) + place] = chosen

    def forward(part):
        for way in range(2):
            by_row[part][way].wait_recv()
            by_col[part][2 * way].start()

    for t in GROUPS[0]:
        tabulate(t, 1, 6 * ROWS - 1)
    forward(0)
    for t in GROUPS[1]:
        tabulate(t, 0, 8 * ROWS - 1)
    forward(1)
    put_in_order(0)
    put_in_order(1)
    for copy in own_p:
        copy.wait()
    for t in range(tiles):
        turned = near[(1 + t % rows_y) * ROWS + 2 + t // rows_y].T
        p_turned[t] = jnp.concatenate([turned, turned], axis=1)
    own_a.wait()
    for i in range(8):
        sums[i][0] = jnp.zeros((tile, tile), F32)
    for group in range(2):
        totals[group][0] = jnp.zeros(totals[group].shape[1:], F32)
    forward(2)
    forward(3)
    for part in (0, 2):
        for piece in (1, 0, 2):
            by_col[part][piece].wait_recv()
    widen.start()

    def multiply(group, tiles_g):
        count = len(GROUPS[group])
        ts = [order[group * count + i] for i in range(count)]
        total_refs = totals[group]
        for i in range(count + 1):
            if i < count:
                total = None
                for place in range(slots):
                    at = ts[i] * slots + place
                    term = dot(a_tiles[pick_a[at]], tiles_g[pick_g[at]])
                    total = term if total is None else total + term
                    sums[group * count + i][place + 1] = total
            if i > 0:
                t = ts[i - 1]
                own_sums = sums[group * count + i - 1]
                highs, lows = [], []
                for j in range(CSLOTS):
                    base = t * (CSLOTS + 1) + j
                    high, low = split(own_sums[ends[base + 1]] - own_sums[ends[base]])
                    highs.append(high)
                    lows.append(low)
                stacked = jnp.concatenate(
                    [jnp.concatenate(highs, axis=1), jnp.concatenate(lows, axis=1)], axis=0
                )
                total_refs[i] = total_refs[i - 1] + dot(p_turned[t], stacked)

    multiply(0, near)
    for part in (1, 3):
        for piece in (1, 0, 2):
            by_col[part][piece].wait_recv()
    widen.wait()
    multiply(1, wide)

    def of_side(side):
        value = None
        for group in range(2):
            at = group * (SIDES + 1) + side
            part = totals[group][side_ends[at + 1]] - totals[group][side_ends[at]]
            value = part if value is None else value + part
        return value

    leave = []
    for partner in range(2):
        side = (2 * core, 2 - 2 * core)[partner]
        value = of_side(side).astype(BF16)
        for j in range(CSLOTS):
            away[partner, j] = value[:, j * tile:(j + 1) * tile]
        copy = pltpu.make_async_remote_copy(
            src_ref=away.at[partner],
            dst_ref=arrived.at[partner],
            send_sem=away_send.at[partner],
            recv_sem=away_recv.at[partner],
            device_id=(dom, (outer, inner)[partner]),
            device_id_type=MESH,
        )
        copy.start()
        leave.append(copy)
    value = of_side(1)
    for j in range(CSLOTS):
        here[j] = value[:, j * tile:(j + 1) * tile]

    for part in range(4):
        for way in range(2):
            by_row[part][way].wait_send()
        for piece in range(3):
            by_col[part][piece].wait_send()
    for copy in leave:
        copy.wait()


def body(n_dom, n_col, a_tiles, p_tiles, a_cols, slot_map, aggregate):
    rows_x, rows_y, slots, tile, _ = a_tiles.shape
    tiles = rows_x * rows_y
    across = CSLOTS * tile
    any_space = pl.BlockSpec(memory_space=pl.ANY)
    operands = (a_cols, slot_map, aggregate, a_tiles.reshape(tiles * slots, tile, tile), p_tiles)
    here, arrived = pl.pallas_call(
        functools.partial(kernel, n_dom, n_col),
        out_shape=(
            pltpu.VMEM((CSLOTS, tile, tile), F32),
            pltpu.VMEM((2, CSLOTS, tile, tile), BF16),
        ),
        in_specs=[any_space] * 5,
        out_specs=(pl.BlockSpec(memory_space=pltpu.VMEM), any_space),
        scratch_shapes=[
            pltpu.VMEM((tiles * slots, tile, tile), BF16),
            pltpu.VMEM((6 * ROWS, tile, tile), BF16),
            pltpu.VMEM((8 * ROWS, tile, tile), BF16),
            pltpu.VMEM((tiles, tile, 2 * tile), BF16),
        ]
        + [pltpu.VMEM((slots + 1, tile, tile), F32)] * tiles
        + [pltpu.VMEM((tiles // 2 + 1, tile, across), F32)] * 2
        + [
            pltpu.SMEM(a_cols.shape, jnp.int32),
            pltpu.SMEM(slot_map.shape, jnp.int32),
            pltpu.SMEM(aggregate.shape, jnp.int32),
            pltpu.VMEM((2, CSLOTS, tile, tile), BF16),
            pltpu.SMEM((tiles * slots,), jnp.int32),
            pltpu.SMEM((tiles * slots,), jnp.int32),
            pltpu.SMEM((tiles * (CSLOTS + 1),), jnp.int32),
            pltpu.SMEM((tiles,), jnp.int32),
            pltpu.SMEM((2 * (SIDES + 1),), jnp.int32),
            pltpu.SemaphoreType.DMA((6,)),
            pltpu.SemaphoreType.DMA((3,)),
            pltpu.SemaphoreType.DMA((8,)),
            pltpu.SemaphoreType.DMA((8,)),
            pltpu.SemaphoreType.DMA((12,)),
            pltpu.SemaphoreType.DMA((12,)),
            pltpu.SemaphoreType.DMA((2,)),
            pltpu.SemaphoreType.DMA((2,)),
        ],
        compiler_params=pltpu.CompilerParams(
            collective_id=0, has_side_effects=True, vmem_limit_bytes=24 * 2**20
        ),
    )(*(pltpu.with_memory_space_constraint(operand, pltpu.HBM) for operand in operands))
    result = here + arrived[0].astype(F32) + arrived[1].astype(F32)
    return result[None, None]


def solution(mesh):
    in_specs = (
        P("dom", "col", None, None, None),
        P("dom", "col", None, None),
        P("dom", "col", None),
        P("dom", "col", None),
        P("dom", "col"),
    )
    out_specs = P("dom", "col", None, None, None)
    call = functools.partial(body, mesh.shape["dom"], mesh.shape["col"])
    return jax.shard_map(call, mesh=mesh, in_specs=in_specs, out_specs=out_specs, check_vma=False)
```

```python
import functools

import jax
import jax.numpy as jnp
from jax import lax
from jax.experimental import pallas as pl
from jax.experimental.pallas import tpu as pltpu
from jax.sharding import PartitionSpec as P

CSLOTS = 4
SIDES = 3
ROWS = 6
GROUPS = ((1, 2, 5, 6), (0, 3, 4, 7))
MESH = pl.DeviceIdType.MESH
F32 = jnp.float32
BF16 = jnp.bfloat16


def dot(left, right):
    return lax.dot_general(left, right, (((1,), (0,)), ((), ())), preferred_element_type=F32)


def given(*conditions):
    conditions = [condition for condition in conditions if condition is not None]
    return pl.when(functools.reduce(jnp.logical_and, conditions)) if conditions else lambda step: step()


def split(value):
    high = value.astype(BF16)
    return high, (value - high.astype(F32)).astype(BF16)


def kernel(
    n_dom, n_col, a_cols_hbm, slot_map_hbm, aggregate_hbm, a_hbm, p_hbm, here, arrived,
    a_tiles, near, wide, p_turned, *scratch,
):
    sums, totals = scratch[:8], scratch[8:10]
    (
        a_cols, slot_map, aggregate, away, pick_a, pick_g, ends, order, side_ends,
        own_sem, small_sem, row_send, row_recv, col_send, col_recv, away_send, away_recv,
    ) = scratch[10:]
    rows_x, rows_y, slots = a_cols.shape
    tiles = rows_x * rows_y
    tile = p_hbm.shape[-1]
    dom, col = lax.axis_index("dom"), lax.axis_index("col")
    core = lax.rem(col, 2)
    outer, inner = col + 2 * core - 1, col + 1 - 2 * core
    has_up, has_down = dom < n_dom - 1, dom > 0
    has_outer = (outer >= 0) & (outer < n_col)
    takes, gives = (has_up, has_down), (has_down, has_up)
    holds = (has_down, None, has_up)
    columns = (3 * core, 1 + core, 3 - 3 * core, 2 - core)
    landing = (5 - 5 * core, 7 - 7 * core, 5 * core, 7 * core)

    own_p = [
        pltpu.make_async_copy(p_hbm.at[:, y], near.at[pl.ds((y + 1) * ROWS + 2, 2)], own_sem.at[y])
        for y in range(rows_y)
    ]
    own_a = pltpu.make_async_copy(a_hbm, a_tiles, own_sem.at[4])
    widen = pltpu.make_async_copy(near, wide.at[pl.ds(ROWS, 6 * ROWS)], own_sem.at[5])
    for copy in own_p:
        copy.start()
    own_a.start()
    small = [
        pltpu.make_async_copy(source, target, small_sem.at[i])
        for i, (source, target) in enumerate(
            ((a_cols_hbm, a_cols), (slot_map_hbm, slot_map), (aggregate_hbm, aggregate))
        )
    ]
    for copy in small:
        copy.start()

    barrier = pltpu.get_barrier_semaphore()
    for exists, target in (
        (has_up, (dom + 1, col)), (has_down, (dom - 1, col)), (has_outer, (dom, outer)), (None, (dom, inner))
    ):
        given(exists)(
            functools.partial(
                pl.semaphore_signal, barrier, inc=1, device_id=target, device_id_type=MESH
            )
        )
    neighbours = 1 + has_up.astype(jnp.int32) + has_down.astype(jnp.int32) + has_outer.astype(jnp.int32)
    pl.semaphore_wait(barrier, neighbours)

    def along_dom(part, way):
        index = part * 2 + way
        return pltpu.make_async_remote_copy(
            src_ref=p_hbm.at[:, columns[part]],
            dst_ref=near.at[pl.ds((columns[part] + 1) * ROWS + 4 * way, 2)],
            send_sem=row_send.at[index],
            recv_sem=row_recv.at[index],
            device_id=(dom + 1 - 2 * way, col),
            device_id_type=MESH,
        )

    def along_col(part, piece):
        index = part * 3 + piece
        if piece == 1:
            source = p_hbm.at[:, columns[part]]
        else:
            source = near.at[pl.ds((columns[part] + 1) * ROWS + 2 * piece, 2)]
        target = near if part % 2 == 0 else wide
        return pltpu.make_async_remote_copy(
            src_ref=source,
            dst_ref=target.at[pl.ds(landing[part] * ROWS + 2 * piece, 2)],
            send_sem=col_send.at[index],
            recv_sem=col_recv.at[index],
            device_id=(dom, (outer, outer, inner, inner)[part]),
            device_id_type=MESH,
        )

    by_row = [[along_dom(part, way) for way in range(2)] for part in range(4)]
    by_col = [[along_col(part, piece) for piece in range(3)] for part in range(4)]
    partners = (has_outer, has_outer, None, None)
    for part in range(4):
        for way in range(2):
            given(takes[way])(by_row[part][way].start)
        given(partners[part])(by_col[part][1].start)

    for copy in small:
        copy.wait()

    width_y = rows_y * n_col
    origin = (dom * rows_x - 2) * width_y + col * rows_y - 2
    inverse = -(-65536 // width_y)

    def tabulate(t, first_column, most):
        x, y = t // rows_y, t % rows_y
        spots, groups = [], []
        for k in range(slots):
            where = a_cols[x, y, k]
            offset = where - origin
            near_x = (offset * inverse) >> 16
            spot = (offset - near_x * width_y - first_column) * ROWS + near_x
            spots.append(jnp.clip(spot, 0, most))
            groups.append(jnp.where(where >= 0, slot_map[x, y, k], CSLOTS))
        count = jnp.int32(0)
        places = [jnp.int32(-1)] * slots
        ends[t * (CSLOTS + 1)] = 0
        for j in range(CSLOTS):
            for k in range(slots):
                member = groups[k] == j
                places[k] = jnp.where(member, count, places[k])
                count = count + member.astype(jnp.int32)
            ends[t * (CSLOTS + 1) + j + 1] = count
        for place in range(slots):
            slot, spot = jnp.int32(0), jnp.int32((y + 2 - first_column) * ROWS + x + 2)
            for k in range(slots):
                chosen = places[k] == place
                slot = jnp.where(chosen, k, slot)
                spot = jnp.where(chosen, spots[k], spot)
            pick_a[t * slots + place] = t * slots + slot
            pick_g[t * slots + place] = spot

    def put_in_order(group):
        members = GROUPS[group]
        sides = [
            lax.rem(aggregate[t // rows_y, t % rows_y], n_col) - col + 1 for t in members
        ]
        count = jnp.int32(0)
        places = [jnp.int32(0)] * len(members)
        side_ends[group * (SIDES + 1)] = 0
        for side in range(SIDES):
            for i in range(len(members)):
                member = sides[i] == side
                places[i] = jnp.where(member, count, places[i])
                count = count + member.astype(jnp.int32)
            side_ends[group * (SIDES + 1) + side + 1] = count
        for place in range(len(members)):
            chosen = jnp.int32(members[0])
            for i, t in enumerate(members):
                chosen = jnp.where(places[i] == place, t, chosen)
            order[group * len(members) + place] = chosen

    def forward(part):
        for way in range(2):
            @given(gives[way])
            def _():
                by_row[part][way].wait_recv()
                given(partners[part])(by_col[part][2 * way].start)

    for t in GROUPS[0]:
        tabulate(t, 1, 6 * ROWS - 1)
    forward(0)
    for t in GROUPS[1]:
        tabulate(t, 0, 8 * ROWS - 1)
    forward(1)
    put_in_order(0)
    put_in_order(1)
    for copy in own_p:
        copy.wait()
    for t in range(tiles):
        turned = near[(1 + t % rows_y) * ROWS + 2 + t // rows_y].T
        p_turned[t] = jnp.concatenate([turned, turned], axis=1)
    own_a.wait()
    for i in range(8):
        sums[i][0] = jnp.zeros((tile, tile), F32)
    for group in range(2):
        totals[group][0] = jnp.zeros(totals[group].shape[1:], F32)
    forward(2)
    forward(3)
    for part in (0, 2):
        for piece in (1, 0, 2):
            given(partners[part], holds[piece])(by_col[part][piece].wait_recv)
    widen.start()

    def multiply(group, tiles_g):
        count = len(GROUPS[group])
        ts = [order[group * count + i] for i in range(count)]
        total_refs = totals[group]
        for i in range(count + 1):
            if i < count:
                total = None
                for place in range(slots):
                    at = ts[i] * slots + place
                    term = dot(a_tiles[pick_a[at]], tiles_g[pick_g[at]])
                    total = term if total is None else total + term
                    sums[group * count + i][place + 1] = total
            if i > 0:
                t = ts[i - 1]
                own_sums = sums[group * count + i - 1]
                highs, lows = [], []
                for j in range(CSLOTS):
                    base = t * (CSLOTS + 1) + j
                    high, low = split(own_sums[ends[base + 1]] - own_sums[ends[base]])
                    highs.append(high)
                    lows.append(low)
                stacked = jnp.concatenate(
                    [jnp.concatenate(highs, axis=1), jnp.concatenate(lows, axis=1)], axis=0
                )
                total_refs[i] = total_refs[i - 1] + dot(p_turned[t], stacked)

    multiply(0, near)
    for part in (1, 3):
        for piece in (1, 0, 2):
            given(partners[part], holds[piece])(by_col[part][piece].wait_recv)
    widen.wait()
    multiply(1, wide)

    def of_side(side):
        value = None
        for group in range(2):
            at = group * (SIDES + 1) + side
            part = totals[group][side_ends[at + 1]] - totals[group][side_ends[at]]
            value = part if value is None else value + part
        return value

    leave = []
    kept = pltpu.make_async_copy(away.at[0], arrived.at[0], own_sem.at[6])
    for partner in range(2):
        side = (2 * core, 2 - 2 * core)[partner]
        value = of_side(side).astype(BF16)
        for j in range(CSLOTS):
            away[partner, j] = value[:, j * tile:(j + 1) * tile]
        copy = pltpu.make_async_remote_copy(
            src_ref=away.at[partner],
            dst_ref=arrived.at[partner],
            send_sem=away_send.at[partner],
            recv_sem=away_recv.at[partner],
            device_id=(dom, (outer, inner)[partner]),
            device_id_type=MESH,
        )
        given((has_outer, None)[partner])(copy.start)
        leave.append(copy)
    given(jnp.logical_not(has_outer))(kept.start)
    value = of_side(1)
    for j in range(CSLOTS):
        here[j] = value[:, j * tile:(j + 1) * tile]

    for part in range(4):
        for way in range(2):
            given(takes[way])(by_row[part][way].wait_send)
        for piece in range(3):
            given(partners[part], holds[piece])(by_col[part][piece].wait_send)
    leave[1].wait()
    given(has_outer)(leave[0].wait)
    given(jnp.logical_not(has_outer))(kept.wait)


def body(n_dom, n_col, a_tiles, p_tiles, a_cols, slot_map, aggregate):
    rows_x, rows_y, slots, tile, _ = a_tiles.shape
    tiles = rows_x * rows_y
    across = CSLOTS * tile
    any_space = pl.BlockSpec(memory_space=pl.ANY)
    operands = (a_cols, slot_map, aggregate, a_tiles.reshape(tiles * slots, tile, tile), p_tiles)
    here, arrived = pl.pallas_call(
        functools.partial(kernel, n_dom, n_col),
        out_shape=(
            pltpu.VMEM((CSLOTS, tile, tile), F32),
            pltpu.VMEM((2, CSLOTS, tile, tile), BF16),
        ),
        in_specs=[any_space] * 5,
        out_specs=(pl.BlockSpec(memory_space=pltpu.VMEM), any_space),
        scratch_shapes=[
            pltpu.VMEM((tiles * slots, tile, tile), BF16),
            pltpu.VMEM((6 * ROWS, tile, tile), BF16),
            pltpu.VMEM((8 * ROWS, tile, tile), BF16),
            pltpu.VMEM((tiles, tile, 2 * tile), BF16),
        ]
        + [pltpu.VMEM((slots + 1, tile, tile), F32)] * tiles
        + [pltpu.VMEM((tiles // 2 + 1, tile, across), F32)] * 2
        + [
            pltpu.SMEM(a_cols.shape, jnp.int32),
            pltpu.SMEM(slot_map.shape, jnp.int32),
            pltpu.SMEM(aggregate.shape, jnp.int32),
            pltpu.VMEM((2, CSLOTS, tile, tile), BF16),
            pltpu.SMEM((tiles * slots,), jnp.int32),
            pltpu.SMEM((tiles * slots,), jnp.int32),
            pltpu.SMEM((tiles * (CSLOTS + 1),), jnp.int32),
            pltpu.SMEM((tiles,), jnp.int32),
            pltpu.SMEM((2 * (SIDES + 1),), jnp.int32),
            pltpu.SemaphoreType.DMA((7,)),
            pltpu.SemaphoreType.DMA((3,)),
            pltpu.SemaphoreType.DMA((8,)),
            pltpu.SemaphoreType.DMA((8,)),
            pltpu.SemaphoreType.DMA((12,)),
            pltpu.SemaphoreType.DMA((12,)),
            pltpu.SemaphoreType.DMA((2,)),
            pltpu.SemaphoreType.DMA((2,)),
        ],
        compiler_params=pltpu.CompilerParams(
            collective_id=0, has_side_effects=True, vmem_limit_bytes=24 * 2**20
        ),
    )(*(pltpu.with_memory_space_constraint(operand, pltpu.HBM) for operand in operands))
    result = here + arrived[0].astype(F32) + arrived[1].astype(F32)
    return result[None, None]


def solution(mesh):
    in_specs = (
        P("dom", "col", None, None, None),
        P("dom", "col", None, None),
        P("dom", "col", None),
        P("dom", "col", None),
        P("dom", "col"),
    )
    out_specs = P("dom", "col", None, None, None)
    call = functools.partial(body, mesh.shape["dom"], mesh.shape["col"])
    return jax.shard_map(call, mesh=mesh, in_specs=in_specs, out_specs=out_specs, check_vma=False)
```

```python
import functools

import jax
import jax.numpy as jnp
from jax import lax
from jax.experimental import pallas as pl
from jax.experimental.pallas import tpu as pltpu
from jax.sharding import PartitionSpec as P

CSLOTS = 4
SIDES = 3
ROWS = 6
NEAR = 6 * ROWS
GROUPS = (4, 2, 2)
MESH = pl.DeviceIdType.MESH
F32 = jnp.float32
BF16 = jnp.bfloat16


def dot(left, right):
    return lax.dot_general(left, right, (((1,), (0,)), ((), ())), preferred_element_type=F32)


def given(*conditions):
    conditions = [condition for condition in conditions if condition is not None]
    return pl.when(functools.reduce(jnp.logical_and, conditions)) if conditions else lambda step: step()


def split(value):
    high = value.astype(BF16)
    return high, (value - high.astype(F32)).astype(BF16)


def kernel(
    n_dom, n_col, a_cols_hbm, slot_map_hbm, aggregate_hbm, a_hbm, p_hbm, here, arrived,
    a_tiles, near, far_outer, far_inner, p_turned, *scratch,
):
    sums, totals = scratch[:8], scratch[8:11]
    (
        a_cols, slot_map, aggregate, away, pick_a, pick_g, ends, order, side_ends,
        ready, own_sem, small_sem, row_send, row_recv, col_send, col_recv, away_send, away_recv,
    ) = scratch[11:]
    rows_x, rows_y, slots = a_cols.shape
    tiles = rows_x * rows_y
    tile = p_hbm.shape[-1]
    dom, col = lax.axis_index("dom"), lax.axis_index("col")
    core = lax.rem(col, 2)
    outer, inner = col + 2 * core - 1, col + 1 - 2 * core
    has_up, has_down = dom < n_dom - 1, dom > 0
    has_outer = (outer >= 0) & (outer < n_col)
    takes, gives = (has_up, has_down), (has_down, has_up)
    holds = (has_down, None, has_up)
    columns = (3 * core, 1 + core, 3 - 3 * core, 2 - core)
    landing = (5 - 5 * core, 0, 5 * core, 0)
    members = ((1, 2, 5, 6), (3 * core, 3 * core + 4), (3 - 3 * core, 7 - 3 * core))

    barrier = pltpu.get_barrier_semaphore()
    is_first, is_second = core == 0, core == 1

    def tell(semaphore, target, *conditions):
        given(*conditions)(
            functools.partial(
                pl.semaphore_signal, semaphore, inc=1, device_id=target, device_id_type=MESH
            )
        )

    tell(barrier, (dom + 1, col), has_up, dom > 0)
    tell(barrier, (dom - 1, col), has_down)
    tell(barrier, (dom, inner), col > 0)
    tell(barrier, (dom, outer), has_outer, is_second)
    own_p = [
        pltpu.make_async_copy(p_hbm.at[:, y], near.at[pl.ds((y + 1) * ROWS + 2, 2)], own_sem.at[y])
        for y in range(rows_y)
    ]
    own_a = pltpu.make_async_copy(a_hbm, a_tiles, own_sem.at[4])
    for copy in own_p:
        copy.start()
    own_a.start()
    small = [
        pltpu.make_async_copy(source, target, small_sem.at[i])
        for i, (source, target) in enumerate(
            ((a_cols_hbm, a_cols), (slot_map_hbm, slot_map), (aggregate_hbm, aggregate))
        )
    ]
    for copy in small:
        copy.start()

    heard = (dom > 1, has_up, col != 1, has_outer & is_first)
    pl.semaphore_wait(barrier, sum(condition.astype(jnp.int32) for condition in heard))
    tell(ready.at[0], (dom + 1, col), dom == 0)
    tell(ready.at[1], (dom, inner), col == 0)
    tell(ready.at[2], (dom, outer), has_outer, is_first)

    def along_dom(part, way):
        index = part * 2 + way
        return pltpu.make_async_remote_copy(
            src_ref=p_hbm.at[:, columns[part]],
            dst_ref=near.at[pl.ds((columns[part] + 1) * ROWS + 4 * way, 2)],
            send_sem=row_send.at[index],
            recv_sem=row_recv.at[index],
            device_id=(dom + 1 - 2 * way, col),
            device_id_type=MESH,
        )

    def along_col(part, piece):
        index = part * 3 + piece
        if piece == 1:
            source = p_hbm.at[:, columns[part]]
        else:
            source = near.at[pl.ds((columns[part] + 1) * ROWS + 2 * piece, 2)]
        target = (near, far_outer, near, far_inner)[part]
        return pltpu.make_async_remote_copy(
            src_ref=source,
            dst_ref=target.at[pl.ds(landing[part] * ROWS + 2 * piece, 2)],
            send_sem=col_send.at[index],
            recv_sem=col_recv.at[index],
            device_id=(dom, (outer, outer, inner, inner)[part]),
            device_id_type=MESH,
        )

    by_row = [[along_dom(part, way) for way in range(2)] for part in range(4)]
    by_col = [[along_col(part, piece) for piece in range(3)] for part in range(4)]
    partners = (has_outer, has_outer, None, None)
    at_once = ((has_outer & is_first,) * 2) + ((col != 1,) * 2)
    for part in range(4):
        given(has_up)(by_row[part][0].start)
        given(dom > 1)(by_row[part][1].start)
        given(at_once[part])(by_col[part][1].start)

    @pl.when(dom == 1)
    def _():
        pl.semaphore_wait(ready.at[0], 1)
        for part in range(4):
            by_row[part][1].start()


    for copy in small:
        copy.wait()

    width_y = rows_y * n_col
    origin = (dom * rows_x - 2) * width_y + col * rows_y - 2
    inverse = -(-65536 // width_y)

    def tabulate(t):
        x, y = t // rows_y, lax.rem(t, rows_y)
        spots, groups = [], []
        for k in range(slots):
            where = a_cols[x, y, k]
            offset = where - origin
            near_x = (offset * inverse) >> 16
            near_y = offset - near_x * width_y
            spot = jnp.where((near_y == 0) | (near_y == 7), NEAR + near_x, (near_y - 1) * ROWS + near_x)
            spots.append(jnp.clip(spot, 0, NEAR + ROWS - 1))
            groups.append(jnp.where(where >= 0, slot_map[x, y, k], CSLOTS))
        count = jnp.int32(0)
        places = [jnp.int32(-1)] * slots
        ends[t * (CSLOTS + 1)] = 0
        for j in range(CSLOTS):
            for k in range(slots):
                member = groups[k] == j
                places[k] = jnp.where(member, count, places[k])
                count = count + member.astype(jnp.int32)
            ends[t * (CSLOTS + 1) + j + 1] = count
        for place in range(slots):
            slot, spot = jnp.int32(0), jnp.int32((y + 1) * ROWS + x + 2)
            for k in range(slots):
                chosen = places[k] == place
                slot = jnp.where(chosen, k, slot)
                spot = jnp.where(chosen, spots[k], spot)
            pick_a[t * slots + place] = t * slots + slot
            pick_g[t * slots + place] = spot

    def put_in_order(group):
        ts, first = members[group], sum(GROUPS[:group])
        sides = [lax.rem(aggregate[t // rows_y, lax.rem(t, rows_y)], n_col) - col + 1 for t in ts]
        count = jnp.int32(0)
        places = [jnp.int32(0)] * len(ts)
        side_ends[group * (SIDES + 1)] = 0
        for side in range(SIDES):
            for i in range(len(ts)):
                member = sides[i] == side
                places[i] = jnp.where(member, count, places[i])
                count = count + member.astype(jnp.int32)
            side_ends[group * (SIDES + 1) + side + 1] = count
        for place in range(len(ts)):
            chosen = jnp.int32(ts[0])
            for i, t in enumerate(ts):
                chosen = jnp.where(places[i] == place, t, chosen)
            order[first + place] = chosen

    def forward(part):
        for way in range(2):
            @given(gives[way])
            def _():
                by_row[part][way].wait_recv()
                given(partners[part])(by_col[part][2 * way].start)

    for t in members[0]:
        tabulate(t)

    @pl.when(has_outer & is_second)
    def _():
        pl.semaphore_wait(ready.at[2], 1)
        for part in range(2):
            by_col[part][1].start()

    forward(0)
    for t in members[1] + members[2]:
        tabulate(t)
    forward(1)
    for group in range(3):
        put_in_order(group)
    for copy in own_p:
        copy.wait()
    for t in range(tiles):
        turned = near[(1 + t % rows_y) * ROWS + 2 + t // rows_y].T
        p_turned[t] = jnp.concatenate([turned, turned], axis=1)
    own_a.wait()
    for i in range(8):
        sums[i][0] = jnp.zeros((tile, tile), F32)
    for group in range(3):
        totals[group][0] = jnp.zeros(totals[group].shape[1:], F32)

    @pl.when(col == 1)
    def _():
        pl.semaphore_wait(ready.at[1], 1)
        for part in (2, 3):
            by_col[part][1].start()

    forward(2)
    forward(3)
    for part in (0, 2):
        for piece in (1, 0, 2):
            given(partners[part], holds[piece])(by_col[part][piece].wait_recv)

    ts = [order[i] for i in range(tiles)]

    def slot_sums(i, far):
        total = None
        for place in range(slots):
            at = ts[i] * slots + place
            spot = pick_g[at]
            if far is None:
                right = near[jnp.minimum(spot, NEAR - 1)]
            else:
                right = jnp.where(
                    spot >= NEAR, far[jnp.maximum(spot - NEAR, 0)], near[jnp.minimum(spot, NEAR - 1)]
                )
            term = dot(a_tiles[pick_a[at]], right)
            total = term if total is None else total + term
            sums[i][place + 1] = total

    def coarse_sums(i, group):
        place = i - sum(GROUPS[:group])
        t = ts[i]
        highs, lows = [], []
        for j in range(CSLOTS):
            base = t * (CSLOTS + 1) + j
            high, low = split(sums[i][ends[base + 1]] - sums[i][ends[base]])
            highs.append(high)
            lows.append(low)
        stacked = jnp.concatenate(
            [jnp.concatenate(highs, axis=1), jnp.concatenate(lows, axis=1)], axis=0
        )
        totals[group][place + 1] = totals[group][place] + dot(p_turned[t], stacked)

    group_of = [group for group, size in enumerate(GROUPS) for _ in range(size)]
    for i in range(tiles + 1):
        if i == GROUPS[0]:
            for piece in (1, 0, 2):
                given(has_outer, holds[piece])(by_col[1][piece].wait_recv)
        if i == GROUPS[0] + GROUPS[1]:
            for piece in (1, 0, 2):
                given(holds[piece])(by_col[3][piece].wait_recv)
        if i < tiles:
            slot_sums(i, (None, far_outer, far_inner)[group_of[i]])
        if i > 0:
            coarse_sums(i - 1, group_of[i - 1])

    def of_side(side):
        value = None
        for group in range(3):
            at = group * (SIDES + 1) + side
            part = totals[group][side_ends[at + 1]] - totals[group][side_ends[at]]
            value = part if value is None else value + part
        return value

    leave = []
    kept = pltpu.make_async_copy(away.at[0], arrived.at[0], own_sem.at[5])
    for partner in range(2):
        side = (2 * core, 2 - 2 * core)[partner]
        value = of_side(side).astype(BF16)
        for j in range(CSLOTS):
            away[partner, j] = value[:, j * tile:(j + 1) * tile]
        copy = pltpu.make_async_remote_copy(
            src_ref=away.at[partner],
            dst_ref=arrived.at[partner],
            send_sem=away_send.at[partner],
            recv_sem=away_recv.at[partner],
            device_id=(dom, (outer, inner)[partner]),
            device_id_type=MESH,
        )
        given((has_outer, None)[partner])(copy.start)
        leave.append(copy)
    given(jnp.logical_not(has_outer))(kept.start)
    value = of_side(1)
    for j in range(CSLOTS):
        here[j] = value[:, j * tile:(j + 1) * tile]

    for part in range(4):
        for way in range(2):
            given(takes[way])(by_row[part][way].wait_send)
        for piece in range(3):
            given(partners[part], holds[piece])(by_col[part][piece].wait_send)
    leave[1].wait()
    given(has_outer)(leave[0].wait)
    given(jnp.logical_not(has_outer))(kept.wait)


def body(n_dom, n_col, a_tiles, p_tiles, a_cols, slot_map, aggregate):
    rows_x, rows_y, slots, tile, _ = a_tiles.shape
    tiles = rows_x * rows_y
    across = CSLOTS * tile
    any_space = pl.BlockSpec(memory_space=pl.ANY)
    operands = (a_cols, slot_map, aggregate, a_tiles.reshape(tiles * slots, tile, tile), p_tiles)
    here, arrived = pl.pallas_call(
        functools.partial(kernel, n_dom, n_col),
        out_shape=(
            pltpu.VMEM((CSLOTS, tile, tile), F32),
            pltpu.VMEM((2, CSLOTS, tile, tile), BF16),
        ),
        in_specs=[any_space] * 5,
        out_specs=(pl.BlockSpec(memory_space=pltpu.VMEM), any_space),
        scratch_shapes=[
            pltpu.VMEM((tiles * slots, tile, tile), BF16),
            pltpu.VMEM((NEAR, tile, tile), BF16),
            pltpu.VMEM((ROWS, tile, tile), BF16),
            pltpu.VMEM((ROWS, tile, tile), BF16),
            pltpu.VMEM((tiles, tile, 2 * tile), BF16),
        ]
        + [pltpu.VMEM((slots + 1, tile, tile), F32)] * tiles
        + [pltpu.VMEM((size + 1, tile, across), F32) for size in GROUPS]
        + [
            pltpu.SMEM(a_cols.shape, jnp.int32),
            pltpu.SMEM(slot_map.shape, jnp.int32),
            pltpu.SMEM(aggregate.shape, jnp.int32),
            pltpu.VMEM((2, CSLOTS, tile, tile), BF16),
            pltpu.SMEM((tiles * slots,), jnp.int32),
            pltpu.SMEM((tiles * slots,), jnp.int32),
            pltpu.SMEM((tiles * (CSLOTS + 1),), jnp.int32),
            pltpu.SMEM((tiles,), jnp.int32),
            pltpu.SMEM((3 * (SIDES + 1),), jnp.int32),
            pltpu.SemaphoreType.REGULAR((3,)),
            pltpu.SemaphoreType.DMA((6,)),
            pltpu.SemaphoreType.DMA((3,)),
            pltpu.SemaphoreType.DMA((8,)),
            pltpu.SemaphoreType.DMA((8,)),
            pltpu.SemaphoreType.DMA((12,)),
            pltpu.SemaphoreType.DMA((12,)),
            pltpu.SemaphoreType.DMA((2,)),
            pltpu.SemaphoreType.DMA((2,)),
        ],
        compiler_params=pltpu.CompilerParams(
            collective_id=0, has_side_effects=True, vmem_limit_bytes=24 * 2**20
        ),
    )(*(pltpu.with_memory_space_constraint(operand, pltpu.HBM) for operand in operands))
    result = here + arrived[0].astype(F32) + arrived[1].astype(F32)
    return result[None, None]


def solution(mesh):
    in_specs = (
        P("dom", "col", None, None, None),
        P("dom", "col", None, None),
        P("dom", "col", None),
        P("dom", "col", None),
        P("dom", "col"),
    )
    out_specs = P("dom", "col", None, None, None)
    call = functools.partial(body, mesh.shape["dom"], mesh.shape["col"])
    return jax.shard_map(call, mesh=mesh, in_specs=in_specs, out_specs=out_specs, check_vma=False)
```

```python
import functools

import jax
import jax.numpy as jnp
from jax import lax
from jax.experimental import pallas as pl
from jax.experimental.pallas import tpu as pltpu
from jax.sharding import PartitionSpec as P

CSLOTS = 4
SIDES = 3
ROWS = 6
NEAR = 6 * ROWS
GROUPS = (4, 2, 2)
MESH = pl.DeviceIdType.MESH
F32 = jnp.float32
BF16 = jnp.bfloat16


def dot(left, right):
    return lax.dot_general(left, right, (((1,), (0,)), ((), ())), preferred_element_type=F32)


def given(*conditions):
    conditions = [condition for condition in conditions if condition is not None]
    return pl.when(functools.reduce(jnp.logical_and, conditions)) if conditions else lambda step: step()


def split(value):
    high = value.astype(BF16)
    return high, (value - high.astype(F32)).astype(BF16)


def kernel(
    n_dom, n_col, a_cols_hbm, slot_map_hbm, aggregate_hbm, a_hbm, p_hbm, here, arrived,
    a_tiles, near, far_outer, far_inner, p_turned, *scratch,
):
    sums, totals = scratch[:8], scratch[8:11]
    (
        a_cols, slot_map, aggregate, away, pick_a, pick_g, ends, order, side_ends,
        ready, own_sem, small_sem, row_send, row_recv, col_send, col_recv, away_send, away_recv,
    ) = scratch[11:]
    rows_x, rows_y, slots = a_cols.shape
    tiles = rows_x * rows_y
    tile = p_hbm.shape[-1]
    dom, col = lax.axis_index("dom"), lax.axis_index("col")
    core = lax.rem(col, 2)
    outer, inner = col + 2 * core - 1, col + 1 - 2 * core
    has_up, has_down = dom < n_dom - 1, dom > 0
    has_outer = (outer >= 0) & (outer < n_col)
    takes, gives = (has_up, has_down), (has_down, has_up)
    columns = (3 * core, 1 + core, 3 - 3 * core, 2 - core)
    landing = (5 - 5 * core, 0, 5 * core, 0)
    members = ((1, 2, 5, 6), (3 * core, 3 * core + 4), (3 - 3 * core, 7 - 3 * core))

    barrier = pltpu.get_barrier_semaphore()
    is_first, is_second = core == 0, core == 1

    def tell(semaphore, target, *conditions):
        given(*conditions)(
            functools.partial(
                pl.semaphore_signal, semaphore, inc=1, device_id=target, device_id_type=MESH
            )
        )

    tell(barrier, (dom + 1, col), has_up, dom > 0)
    tell(barrier, (dom - 1, col), has_down)
    tell(barrier, (dom, inner), col > 0)
    tell(barrier, (dom, outer), has_outer, is_second)
    own_p = [
        pltpu.make_async_copy(p_hbm.at[:, y], near.at[pl.ds((y + 1) * ROWS + 2, 2)], own_sem.at[0])
        for y in range(rows_y)
    ]
    own_a = pltpu.make_async_copy(a_hbm, a_tiles, own_sem.at[1])
    for copy in own_p:
        copy.start()
    own_a.start()
    small = [
        pltpu.make_async_copy(source, target, small_sem.at[i])
        for i, (source, target) in enumerate(
            ((a_cols_hbm, a_cols), (slot_map_hbm, slot_map), (aggregate_hbm, aggregate))
        )
    ]
    for copy in small:
        copy.start()

    heard = (dom > 1, has_up, col != 1, has_outer & is_first)
    pl.semaphore_wait(barrier, sum(condition.astype(jnp.int32) for condition in heard))
    tell(ready.at[0], (dom + 1, col), dom == 0)
    tell(ready.at[1], (dom, inner), col == 0)
    tell(ready.at[2], (dom, outer), has_outer, is_first)

    def arrive(semaphore, count):
        some = near.at[pl.ds(0, count)]
        pltpu.make_async_copy(some, some, semaphore).wait()

    def arrive_pieces(semaphore, count, *conditions):
        given(has_up & has_down, *conditions)(lambda: arrive(semaphore, 3 * count))
        given(has_up ^ has_down, *conditions)(lambda: arrive(semaphore, 2 * count))

    def along_dom(part, way):
        index = part * 2 + way
        return pltpu.make_async_remote_copy(
            src_ref=p_hbm.at[:, columns[part]],
            dst_ref=near.at[pl.ds((columns[part] + 1) * ROWS + 4 * way, 2)],
            send_sem=row_send.at[way],
            recv_sem=row_recv.at[index],
            device_id=(dom + 1 - 2 * way, col),
            device_id_type=MESH,
        )

    def along_col(part, piece):
        if piece == 1:
            source = p_hbm.at[:, columns[part]]
        else:
            source = near.at[pl.ds((columns[part] + 1) * ROWS + 2 * piece, 2)]
        target = (near, far_outer, near, far_inner)[part]
        return pltpu.make_async_remote_copy(
            src_ref=source,
            dst_ref=target.at[pl.ds(landing[part] * ROWS + 2 * piece, 2)],
            send_sem=col_send.at[part // 2],
            recv_sem=col_recv.at[part],
            device_id=(dom, (outer, outer, inner, inner)[part]),
            device_id_type=MESH,
        )

    by_row = [[along_dom(part, way) for way in range(2)] for part in range(4)]
    by_col = [[along_col(part, piece) for piece in range(3)] for part in range(4)]
    partners = (has_outer, has_outer, None, None)
    at_once = ((has_outer & is_first,) * 2) + ((col != 1,) * 2)
    for part in range(4):
        given(has_up)(by_row[part][0].start)
        given(dom > 1)(by_row[part][1].start)
        given(at_once[part])(by_col[part][1].start)

    @pl.when(dom == 1)
    def _():
        pl.semaphore_wait(ready.at[0], 1)
        for part in range(4):
            by_row[part][1].start()


    for copy in small:
        copy.wait()

    width_y = rows_y * n_col
    origin = (dom * rows_x - 2) * width_y + col * rows_y - 2
    inverse = -(-65536 // width_y)

    def tabulate(t):
        x, y = t // rows_y, lax.rem(t, rows_y)
        spots, groups = [], []
        for k in range(slots):
            where = a_cols[x, y, k]
            offset = where - origin
            near_x = (offset * inverse) >> 16
            near_y = offset - near_x * width_y
            spot = jnp.where((near_y == 0) | (near_y == 7), NEAR + near_x, (near_y - 1) * ROWS + near_x)
            spots.append(jnp.clip(spot, 0, NEAR + ROWS - 1))
            groups.append(jnp.where(where >= 0, slot_map[x, y, k], CSLOTS))
        count = jnp.int32(0)
        places = [jnp.int32(-1)] * slots
        ends[t * (CSLOTS + 1)] = 0
        for j in range(CSLOTS):
            for k in range(slots):
                member = groups[k] == j
                places[k] = jnp.where(member, count, places[k])
                count = count + member.astype(jnp.int32)
            ends[t * (CSLOTS + 1) + j + 1] = count
        for place in range(slots):
            slot, spot = jnp.int32(0), jnp.int32((y + 1) * ROWS + x + 2)
            for k in range(slots):
                chosen = places[k] == place
                slot = jnp.where(chosen, k, slot)
                spot = jnp.where(chosen, spots[k], spot)
            pick_a[t * slots + place] = t * slots + slot
            pick_g[t * slots + place] = spot

    def put_in_order(group):
        ts, first = members[group], sum(GROUPS[:group])
        sides = [lax.rem(aggregate[t // rows_y, lax.rem(t, rows_y)], n_col) - col + 1 for t in ts]
        count = jnp.int32(0)
        places = [jnp.int32(0)] * len(ts)
        side_ends[group * (SIDES + 1)] = 0
        for side in range(SIDES):
            for i in range(len(ts)):
                member = sides[i] == side
                places[i] = jnp.where(member, count, places[i])
                count = count + member.astype(jnp.int32)
            side_ends[group * (SIDES + 1) + side + 1] = count
        for place in range(len(ts)):
            chosen = jnp.int32(ts[0])
            for i, t in enumerate(ts):
                chosen = jnp.where(places[i] == place, t, chosen)
            order[first + place] = chosen

    def forward(part):
        for way in range(2):
            @given(gives[way])
            def _():
                by_row[part][way].wait_recv()
                given(partners[part])(by_col[part][2 * way].start)

    for t in members[0]:
        tabulate(t)

    @pl.when(has_outer & is_second)
    def _():
        pl.semaphore_wait(ready.at[2], 1)
        for part in range(2):
            by_col[part][1].start()

    forward(0)
    for t in members[1] + members[2]:
        tabulate(t)
    forward(1)
    for group in range(3):
        put_in_order(group)
    arrive(own_sem.at[0], tiles)
    for t in range(tiles):
        turned = near[(1 + t % rows_y) * ROWS + 2 + t // rows_y].T
        p_turned[t] = jnp.concatenate([turned, turned], axis=1)
    own_a.wait()
    for i in range(8):
        sums[i][0] = jnp.zeros((tile, tile), F32)
    for group in range(3):
        totals[group][0] = jnp.zeros(totals[group].shape[1:], F32)

    @pl.when(col == 1)
    def _():
        pl.semaphore_wait(ready.at[1], 1)
        for part in (2, 3):
            by_col[part][1].start()

    forward(2)
    forward(3)
    for part in (0, 2):
        arrive_pieces(col_recv.at[part], 2, partners[part])

    ts = [order[i] for i in range(tiles)]

    def slot_sums(i, far):
        total = None
        for place in range(slots):
            at = ts[i] * slots + place
            spot = pick_g[at]
            if far is None:
                right = near[jnp.minimum(spot, NEAR - 1)]
            else:
                right = jnp.where(
                    spot >= NEAR, far[jnp.maximum(spot - NEAR, 0)], near[jnp.minimum(spot, NEAR - 1)]
                )
            term = dot(a_tiles[pick_a[at]], right)
            total = term if total is None else total + term
            sums[i][place + 1] = total

    def coarse_sums(i, group):
        place = i - sum(GROUPS[:group])
        t = ts[i]
        highs, lows = [], []
        for j in range(CSLOTS):
            base = t * (CSLOTS + 1) + j
            high, low = split(sums[i][ends[base + 1]] - sums[i][ends[base]])
            highs.append(high)
            lows.append(low)
        stacked = jnp.concatenate(
            [jnp.concatenate(highs, axis=1), jnp.concatenate(lows, axis=1)], axis=0
        )
        totals[group][place + 1] = totals[group][place] + dot(p_turned[t], stacked)

    group_of = [group for group, size in enumerate(GROUPS) for _ in range(size)]
    for i in range(tiles + 1):
        if i == GROUPS[0]:
            arrive_pieces(col_recv.at[1], 2, has_outer)
        if i == GROUPS[0] + GROUPS[1]:
            arrive_pieces(col_recv.at[3], 2)
        if i < tiles:
            slot_sums(i, (None, far_outer, far_inner)[group_of[i]])
        if i > 0:
            coarse_sums(i - 1, group_of[i - 1])

    def of_side(side):
        value = None
        for group in range(3):
            at = group * (SIDES + 1) + side
            part = totals[group][side_ends[at + 1]] - totals[group][side_ends[at]]
            value = part if value is None else value + part
        return value

    leave = []
    kept = pltpu.make_async_copy(away.at[0], arrived.at[0], own_sem.at[2])
    for partner in range(2):
        side = (2 * core, 2 - 2 * core)[partner]
        value = of_side(side).astype(BF16)
        for j in range(CSLOTS):
            away[partner, j] = value[:, j * tile:(j + 1) * tile]
        copy = pltpu.make_async_remote_copy(
            src_ref=away.at[partner],
            dst_ref=arrived.at[partner],
            send_sem=away_send.at[partner],
            recv_sem=away_recv.at[partner],
            device_id=(dom, (outer, inner)[partner]),
            device_id_type=MESH,
        )
        given((has_outer, None)[partner])(copy.start)
        leave.append(copy)
    given(jnp.logical_not(has_outer))(kept.start)
    value = of_side(1)
    for j in range(CSLOTS):
        here[j] = value[:, j * tile:(j + 1) * tile]

    for way in range(2):
        given(takes[way])(functools.partial(arrive, row_send.at[way], tiles))
    arrive_pieces(col_send.at[0], 4, has_outer)
    arrive_pieces(col_send.at[1], 4)
    leave[1].wait()
    given(has_outer)(leave[0].wait)
    given(jnp.logical_not(has_outer))(kept.wait)


def body(n_dom, n_col, a_tiles, p_tiles, a_cols, slot_map, aggregate):
    rows_x, rows_y, slots, tile, _ = a_tiles.shape
    tiles = rows_x * rows_y
    across = CSLOTS * tile
    any_space = pl.BlockSpec(memory_space=pl.ANY)
    operands = (a_cols, slot_map, aggregate, a_tiles.reshape(tiles * slots, tile, tile), p_tiles)
    here, arrived = pl.pallas_call(
        functools.partial(kernel, n_dom, n_col),
        out_shape=(
            pltpu.VMEM((CSLOTS, tile, tile), F32),
            pltpu.VMEM((2, CSLOTS, tile, tile), BF16),
        ),
        in_specs=[any_space] * 5,
        out_specs=(pl.BlockSpec(memory_space=pltpu.VMEM), any_space),
        scratch_shapes=[
            pltpu.VMEM((tiles * slots, tile, tile), BF16),
            pltpu.VMEM((NEAR, tile, tile), BF16),
            pltpu.VMEM((ROWS, tile, tile), BF16),
            pltpu.VMEM((ROWS, tile, tile), BF16),
            pltpu.VMEM((tiles, tile, 2 * tile), BF16),
        ]
        + [pltpu.VMEM((slots + 1, tile, tile), F32)] * tiles
        + [pltpu.VMEM((size + 1, tile, across), F32) for size in GROUPS]
        + [
            pltpu.SMEM(a_cols.shape, jnp.int32),
            pltpu.SMEM(slot_map.shape, jnp.int32),
            pltpu.SMEM(aggregate.shape, jnp.int32),
            pltpu.VMEM((2, CSLOTS, tile, tile), BF16),
            pltpu.SMEM((tiles * slots,), jnp.int32),
            pltpu.SMEM((tiles * slots,), jnp.int32),
            pltpu.SMEM((tiles * (CSLOTS + 1),), jnp.int32),
            pltpu.SMEM((tiles,), jnp.int32),
            pltpu.SMEM((3 * (SIDES + 1),), jnp.int32),
            pltpu.SemaphoreType.REGULAR((3,)),
            pltpu.SemaphoreType.DMA((3,)),
            pltpu.SemaphoreType.DMA((3,)),
            pltpu.SemaphoreType.DMA((2,)),
            pltpu.SemaphoreType.DMA((8,)),
            pltpu.SemaphoreType.DMA((2,)),
            pltpu.SemaphoreType.DMA((4,)),
            pltpu.SemaphoreType.DMA((2,)),
            pltpu.SemaphoreType.DMA((2,)),
        ],
        compiler_params=pltpu.CompilerParams(
            collective_id=0, has_side_effects=True, vmem_limit_bytes=24 * 2**20
        ),
    )(*(pltpu.with_memory_space_constraint(operand, pltpu.HBM) for operand in operands))
    result = here + arrived[0].astype(F32) + arrived[1].astype(F32)
    return result[None, None]


def solution(mesh):
    in_specs = (
        P("dom", "col", None, None, None),
        P("dom", "col", None, None),
        P("dom", "col", None),
        P("dom", "col", None),
        P("dom", "col"),
    )
    out_specs = P("dom", "col", None, None, None)
    call = functools.partial(body, mesh.shape["dom"], mesh.shape["col"])
    return jax.shard_map(call, mesh=mesh, in_specs=in_specs, out_specs=out_specs, check_vma=False)
```

```python
import functools

import jax
import jax.numpy as jnp
from jax import lax
from jax.experimental import pallas as pl
from jax.experimental.pallas import tpu as pltpu
from jax.sharding import PartitionSpec as P

CSLOTS = 4
SIDES = 3
ROWS = 6
NEAR = 6 * ROWS
GROUPS = (4, 2, 2)
MESH = pl.DeviceIdType.MESH
F32 = jnp.float32
BF16 = jnp.bfloat16


def dot(left, right):
    return lax.dot_general(left, right, (((1,), (0,)), ((), ())), preferred_element_type=F32)


def given(*conditions):
    conditions = [condition for condition in conditions if condition is not None]
    return pl.when(functools.reduce(jnp.logical_and, conditions)) if conditions else lambda step: step()


def split(value):
    high = value.astype(BF16)
    return high, (value - high.astype(F32)).astype(BF16)


def kernel(
    n_dom, n_col, a_cols_hbm, slot_map_hbm, aggregate_hbm, a_hbm, p_hbm, here, arrived,
    a_tiles, near, far_outer, far_inner, relayed, p_turned, *scratch,
):
    sums, totals = scratch[:8], scratch[8:11]
    (
        a_cols, slot_map, aggregate, away, pick_a, pick_g, ends, order, side_ends,
        ready, relay_send, relay_recv, own_sem, small_sem, row_send, row_recv, col_send, col_recv, away_send, away_recv,
    ) = scratch[11:]
    rows_x, rows_y, slots = a_cols.shape
    tiles = rows_x * rows_y
    tile = p_hbm.shape[-1]
    dom, col = lax.axis_index("dom"), lax.axis_index("col")
    core = lax.rem(col, 2)
    outer, inner = col + 2 * core - 1, col + 1 - 2 * core
    has_up, has_down = dom < n_dom - 1, dom > 0
    has_outer = (outer >= 0) & (outer < n_col)
    takes, gives = (has_up, has_down), (has_down, has_up)
    columns = (3 * core, 1 + core, 3 - 3 * core, 2 - core)
    landing = (5 - 5 * core, 0, 5 * core, 0)
    members = ((1, 2, 5, 6), (3 * core, 3 * core + 4), (3 - 3 * core, 7 - 3 * core))

    barrier = pltpu.get_barrier_semaphore()
    is_first, is_second = core == 0, core == 1

    def tell(semaphore, target, *conditions):
        given(*conditions)(
            functools.partial(
                pl.semaphore_signal, semaphore, inc=1, device_id=target, device_id_type=MESH
            )
        )

    is_relay, is_source = (dom == 0) & (col == 1), (dom == 1) & (col == 0)
    tell(barrier, (dom + 1, col), has_up, dom > 0)
    tell(barrier, (dom + 1, inner), is_relay)
    tell(barrier, (dom - 1, col), has_down)
    tell(barrier, (dom, inner), col > 0)
    tell(barrier, (dom, outer), has_outer, is_second)
    own_p = [
        pltpu.make_async_copy(p_hbm.at[:, y], near.at[pl.ds((y + 1) * ROWS + 2, 2)], own_sem.at[0])
        for y in range(rows_y)
    ]
    own_a = pltpu.make_async_copy(a_hbm, a_tiles, own_sem.at[1])
    for copy in own_p:
        copy.start()
    own_a.start()
    small = [
        pltpu.make_async_copy(source, target, small_sem.at[i])
        for i, (source, target) in enumerate(
            ((a_cols_hbm, a_cols), (slot_map_hbm, slot_map), (aggregate_hbm, aggregate))
        )
    ]
    for copy in small:
        copy.start()

    heard = (dom > 1, has_up, col != 1, has_outer & is_first, is_source)
    pl.semaphore_wait(barrier, sum(condition.astype(jnp.int32) for condition in heard))
    tell(ready.at[0], (dom + 1, col), dom == 0, col > 0)
    tell(ready.at[1], (dom, inner), col == 0)
    tell(ready.at[2], (dom, outer), has_outer, is_first)

    def arrive(semaphore, count):
        some = near.at[pl.ds(0, count)]
        pltpu.make_async_copy(some, some, semaphore).wait()

    def arrive_pieces(semaphore, count, *conditions):
        given(has_up & has_down, *conditions)(lambda: arrive(semaphore, 3 * count))
        given(has_up ^ has_down, *conditions)(lambda: arrive(semaphore, 2 * count))

    def along_dom(part, way):
        index = part * 2 + way
        return pltpu.make_async_remote_copy(
            src_ref=p_hbm.at[:, columns[part]],
            dst_ref=near.at[pl.ds((columns[part] + 1) * ROWS + 4 * way, 2)],
            send_sem=row_send.at[way],
            recv_sem=row_recv.at[index],
            device_id=(dom + 1 - 2 * way, col),
            device_id_type=MESH,
        )

    def along_col(part, piece):
        if piece == 1:
            source = p_hbm.at[:, columns[part]]
        else:
            source = near.at[pl.ds((columns[part] + 1) * ROWS + 2 * piece, 2)]
        target = (near, far_outer, near, far_inner)[part]
        return pltpu.make_async_remote_copy(
            src_ref=source,
            dst_ref=target.at[pl.ds(landing[part] * ROWS + 2 * piece, 2)],
            send_sem=col_send.at[part // 2],
            recv_sem=col_recv.at[part],
            device_id=(dom, (outer, outer, inner, inner)[part]),
            device_id_type=MESH,
        )

    def to_relay(part):
        return pltpu.make_async_remote_copy(
            src_ref=p_hbm.at[:, columns[part]],
            dst_ref=relayed.at[pl.ds(2 * part, 2)],
            send_sem=row_send.at[1],
            recv_sem=relay_recv,
            device_id=(dom - 1, inner),
            device_id_type=MESH,
        )

    def hand_on(part):
        theirs = (0, 1, 3, 2)[part]
        return pltpu.make_async_remote_copy(
            src_ref=relayed.at[pl.ds(2 * part, 2)],
            dst_ref=near.at[pl.ds((theirs + 1) * ROWS + 4, 2)],
            send_sem=relay_send,
            recv_sem=row_recv.at[2 * part + 1],
            device_id=(dom, inner),
            device_id_type=MESH,
        )

    by_row = [[along_dom(part, way) for way in range(2)] for part in range(4)]
    by_col = [[along_col(part, piece) for piece in range(3)] for part in range(4)]
    partners = (has_outer, has_outer, None, None)
    at_once = ((has_outer & is_first,) * 2) + ((col != 1,) * 2)
    for part in range(4):
        given(has_up)(by_row[part][0].start)
        given(dom > 1)(by_row[part][1].start)
        given(at_once[part])(by_col[part][1].start)

    @pl.when((dom == 1) & (col > 0))
    def _():
        pl.semaphore_wait(ready.at[0], 1)
        for part in range(4):
            by_row[part][1].start()

    @pl.when(is_source)
    def _():
        for part in range(4):
            to_relay(part).start()


    for copy in small:
        copy.wait()

    width_y = rows_y * n_col
    origin = (dom * rows_x - 2) * width_y + col * rows_y - 2
    inverse = -(-65536 // width_y)

    def tabulate(t):
        x, y = t // rows_y, lax.rem(t, rows_y)
        spots, groups = [], []
        for k in range(slots):
            where = a_cols[x, y, k]
            offset = where - origin
            near_x = (offset * inverse) >> 16
            near_y = offset - near_x * width_y
            spot = jnp.where((near_y == 0) | (near_y == 7), NEAR + near_x, (near_y - 1) * ROWS + near_x)
            spots.append(jnp.clip(spot, 0, NEAR + ROWS - 1))
            groups.append(jnp.where(where >= 0, slot_map[x, y, k], CSLOTS))
        count = jnp.int32(0)
        places = [jnp.int32(-1)] * slots
        ends[t * (CSLOTS + 1)] = 0
        for j in range(CSLOTS):
            for k in range(slots):
                member = groups[k] == j
                places[k] = jnp.where(member, count, places[k])
                count = count + member.astype(jnp.int32)
            ends[t * (CSLOTS + 1) + j + 1] = count
        for place in range(slots):
            slot, spot = jnp.int32(0), jnp.int32((y + 1) * ROWS + x + 2)
            for k in range(slots):
                chosen = places[k] == place
                slot = jnp.where(chosen, k, slot)
                spot = jnp.where(chosen, spots[k], spot)
            pick_a[t * slots + place] = t * slots + slot
            pick_g[t * slots + place] = spot

    def put_in_order(group):
        ts, first = members[group], sum(GROUPS[:group])
        sides = [lax.rem(aggregate[t // rows_y, lax.rem(t, rows_y)], n_col) - col + 1 for t in ts]
        count = jnp.int32(0)
        places = [jnp.int32(0)] * len(ts)
        side_ends[group * (SIDES + 1)] = 0
        for side in range(SIDES):
            for i in range(len(ts)):
                member = sides[i] == side
                places[i] = jnp.where(member, count, places[i])
                count = count + member.astype(jnp.int32)
            side_ends[group * (SIDES + 1) + side + 1] = count
        for place in range(len(ts)):
            chosen = jnp.int32(ts[0])
            for i, t in enumerate(ts):
                chosen = jnp.where(places[i] == place, t, chosen)
            order[first + place] = chosen

    def forward(part):
        for way in range(2):
            @given(gives[way])
            def _():
                by_row[part][way].wait_recv()
                given(partners[part])(by_col[part][2 * way].start)

    for t in members[0]:
        tabulate(t)

    @pl.when(has_outer & is_second)
    def _():
        pl.semaphore_wait(ready.at[2], 1)
        for part in range(2):
            by_col[part][1].start()

    forward(0)
    for t in members[1] + members[2]:
        tabulate(t)
    forward(1)
    for group in range(3):
        put_in_order(group)
    arrive(own_sem.at[0], tiles)
    for t in range(tiles):
        turned = near[(1 + t % rows_y) * ROWS + 2 + t // rows_y].T
        p_turned[t] = jnp.concatenate([turned, turned], axis=1)
    own_a.wait()
    for i in range(8):
        sums[i][0] = jnp.zeros((tile, tile), F32)
    for group in range(3):
        totals[group][0] = jnp.zeros(totals[group].shape[1:], F32)

    @pl.when(col == 1)
    def _():
        pl.semaphore_wait(ready.at[1], 1)
        for part in (2, 3):
            by_col[part][1].start()

    @pl.when(is_relay)
    def _():
        arrive(relay_recv, tiles)
        for part in range(4):
            hand_on(part).start()

    forward(2)
    forward(3)
    for part in (0, 2):
        arrive_pieces(col_recv.at[part], 2, partners[part])

    ts = [order[i] for i in range(tiles)]

    def slot_sums(i, far):
        total = None
        for place in range(slots):
            at = ts[i] * slots + place
            spot = pick_g[at]
            if far is None:
                right = near[jnp.minimum(spot, NEAR - 1)]
            else:
                right = jnp.where(
                    spot >= NEAR, far[jnp.maximum(spot - NEAR, 0)], near[jnp.minimum(spot, NEAR - 1)]
                )
            term = dot(a_tiles[pick_a[at]], right)
            total = term if total is None else total + term
            sums[i][place + 1] = total

    def coarse_sums(i, group):
        place = i - sum(GROUPS[:group])
        t = ts[i]
        highs, lows = [], []
        for j in range(CSLOTS):
            base = t * (CSLOTS + 1) + j
            high, low = split(sums[i][ends[base + 1]] - sums[i][ends[base]])
            highs.append(high)
            lows.append(low)
        stacked = jnp.concatenate(
            [jnp.concatenate(highs, axis=1), jnp.concatenate(lows, axis=1)], axis=0
        )
        totals[group][place + 1] = totals[group][place] + dot(p_turned[t], stacked)

    group_of = [group for group, size in enumerate(GROUPS) for _ in range(size)]
    for i in range(tiles + 1):
        if i == GROUPS[0]:
            arrive_pieces(col_recv.at[1], 2, has_outer)
        if i == GROUPS[0] + GROUPS[1]:
            arrive_pieces(col_recv.at[3], 2)
        if i < tiles:
            slot_sums(i, (None, far_outer, far_inner)[group_of[i]])
        if i > 0:
            coarse_sums(i - 1, group_of[i - 1])

    def of_side(side):
        value = None
        for group in range(3):
            at = group * (SIDES + 1) + side
            part = totals[group][side_ends[at + 1]] - totals[group][side_ends[at]]
            value = part if value is None else value + part
        return value

    leave = []
    kept = pltpu.make_async_copy(away.at[0], arrived.at[0], own_sem.at[2])
    for partner in range(2):
        side = (2 * core, 2 - 2 * core)[partner]
        value = of_side(side).astype(BF16)
        for j in range(CSLOTS):
            away[partner, j] = value[:, j * tile:(j + 1) * tile]
        copy = pltpu.make_async_remote_copy(
            src_ref=away.at[partner],
            dst_ref=arrived.at[partner],
            send_sem=away_send.at[partner],
            recv_sem=away_recv.at[partner],
            device_id=(dom, (outer, inner)[partner]),
            device_id_type=MESH,
        )
        given((has_outer, None)[partner])(copy.start)
        leave.append(copy)
    given(jnp.logical_not(has_outer))(kept.start)
    value = of_side(1)
    for j in range(CSLOTS):
        here[j] = value[:, j * tile:(j + 1) * tile]

    for way in range(2):
        given(takes[way])(functools.partial(arrive, row_send.at[way], tiles))
    given(is_relay)(functools.partial(arrive, relay_send, tiles))
    arrive_pieces(col_send.at[0], 4, has_outer)
    arrive_pieces(col_send.at[1], 4)
    leave[1].wait()
    given(has_outer)(leave[0].wait)
    given(jnp.logical_not(has_outer))(kept.wait)


def body(n_dom, n_col, a_tiles, p_tiles, a_cols, slot_map, aggregate):
    rows_x, rows_y, slots, tile, _ = a_tiles.shape
    tiles = rows_x * rows_y
    across = CSLOTS * tile
    any_space = pl.BlockSpec(memory_space=pl.ANY)
    operands = (a_cols, slot_map, aggregate, a_tiles.reshape(tiles * slots, tile, tile), p_tiles)
    here, arrived = pl.pallas_call(
        functools.partial(kernel, n_dom, n_col),
        out_shape=(
            pltpu.VMEM((CSLOTS, tile, tile), F32),
            pltpu.VMEM((2, CSLOTS, tile, tile), BF16),
        ),
        in_specs=[any_space] * 5,
        out_specs=(pl.BlockSpec(memory_space=pltpu.VMEM), any_space),
        scratch_shapes=[
            pltpu.VMEM((tiles * slots, tile, tile), BF16),
            pltpu.VMEM((NEAR, tile, tile), BF16),
            pltpu.VMEM((ROWS, tile, tile), BF16),
            pltpu.VMEM((ROWS, tile, tile), BF16),
            pltpu.VMEM((tiles, tile, tile), BF16),
            pltpu.VMEM((tiles, tile, 2 * tile), BF16),
        ]
        + [pltpu.VMEM((slots + 1, tile, tile), F32)] * tiles
        + [pltpu.VMEM((size + 1, tile, across), F32) for size in GROUPS]
        + [
            pltpu.SMEM(a_cols.shape, jnp.int32),
            pltpu.SMEM(slot_map.shape, jnp.int32),
            pltpu.SMEM(aggregate.shape, jnp.int32),
            pltpu.VMEM((2, CSLOTS, tile, tile), BF16),
            pltpu.SMEM((tiles * slots,), jnp.int32),
            pltpu.SMEM((tiles * slots,), jnp.int32),
            pltpu.SMEM((tiles * (CSLOTS + 1),), jnp.int32),
            pltpu.SMEM((tiles,), jnp.int32),
            pltpu.SMEM((3 * (SIDES + 1),), jnp.int32),
            pltpu.SemaphoreType.REGULAR((3,)),
            pltpu.SemaphoreType.DMA,
            pltpu.SemaphoreType.DMA,
            pltpu.SemaphoreType.DMA((3,)),
            pltpu.SemaphoreType.DMA((3,)),
            pltpu.SemaphoreType.DMA((2,)),
            pltpu.SemaphoreType.DMA((8,)),
            pltpu.SemaphoreType.DMA((2,)),
            pltpu.SemaphoreType.DMA((4,)),
            pltpu.SemaphoreType.DMA((2,)),
            pltpu.SemaphoreType.DMA((2,)),
        ],
        compiler_params=pltpu.CompilerParams(
            collective_id=0, has_side_effects=True, vmem_limit_bytes=24 * 2**20
        ),
    )(*(pltpu.with_memory_space_constraint(operand, pltpu.HBM) for operand in operands))
    result = here + arrived[0].astype(F32) + arrived[1].astype(F32)
    return result[None, None]


def solution(mesh):
    in_specs = (
        P("dom", "col", None, None, None),
        P("dom", "col", None, None),
        P("dom", "col", None),
        P("dom", "col", None),
        P("dom", "col"),
    )
    out_specs = P("dom", "col", None, None, None)
    call = functools.partial(body, mesh.shape["dom"], mesh.shape["col"])
    return jax.shard_map(call, mesh=mesh, in_specs=in_specs, out_specs=out_specs, check_vma=False)
```

```python
import functools

import jax
import jax.numpy as jnp
from jax import lax
from jax.experimental import pallas as pl
from jax.experimental.pallas import tpu as pltpu
from jax.sharding import PartitionSpec as P

CSLOTS = 4
SIDES = 3
ROWS = 6
NEAR = 6 * ROWS
RING = 8
GROUPS = (4, 2, 2)
MESH = pl.DeviceIdType.MESH
F32 = jnp.float32
BF16 = jnp.bfloat16


def dot(left, right):
    return lax.dot_general(left, right, (((1,), (0,)), ((), ())), preferred_element_type=F32)


def given(*conditions):
    conditions = [condition for condition in conditions if condition is not None]
    return pl.when(functools.reduce(jnp.logical_and, conditions)) if conditions else lambda step: step()


def split(value):
    high = value.astype(BF16)
    return high, (value - high.astype(F32)).astype(BF16)


def kernel(
    n_dom, n_col, a_cols_hbm, slot_map_hbm, aggregate_hbm, a_hbm, p_hbm, here, arrived,
    a_tiles, near, far_outer, far_inner, relayed, p_turned, *scratch,
):
    sums, totals = scratch[:8], scratch[8:11]
    (
        a_cols, slot_map, aggregate, away, pick_a, pick_g, ends, order, side_ends,
        ready, relay_send, relay_recv, own_sem, small_sem, row_send, row_recv, col_send, col_recv, away_send, away_recv,
    ) = scratch[11:]
    rows_x, rows_y, slots = a_cols.shape
    tiles = rows_x * rows_y
    tile = p_hbm.shape[-1]
    dom, col = lax.axis_index("dom"), lax.axis_index("col")
    core = lax.rem(col, 2)
    outer, inner = col + 2 * core - 1, col + 1 - 2 * core
    has_up, has_down = dom < n_dom - 1, dom > 0
    has_outer = (outer >= 0) & (outer < n_col)
    takes, gives = (has_up, has_down), (has_down, has_up)
    columns = (3 * core, 1 + core, 3 - 3 * core, 2 - core)
    landing = (5 - 5 * core, 0, 5 * core, 0)
    members = ((1, 2, 5, 6), (3 * core, 3 * core + 4), (3 - 3 * core, 7 - 3 * core))

    barrier = pltpu.get_barrier_semaphore()
    is_first, is_second = core == 0, core == 1

    def tell(semaphore, target, *conditions):
        given(*conditions)(
            functools.partial(
                pl.semaphore_signal, semaphore, inc=1, device_id=target, device_id_type=MESH
            )
        )

    is_corner, is_relay, is_source = (dom == 0) & (col == 0), (dom == 0) & (col == 1), (dom == 1) & (col == 0)
    turn = lax.rem(dom, RING)
    late_below, late_above = (dom == 1) | (has_up & (turn == RING - 1)), has_up & (turn == 3)
    replies_up = (dom == 0) | ((dom < n_dom - 2) & (turn == RING - 2))
    replies_down = has_down & (turn == 4)
    early_below, early_above = has_down & jnp.logical_not(late_below), has_up & jnp.logical_not(late_above)
    tell(barrier, (dom + 1, col), has_up, jnp.logical_not(replies_up))
    tell(barrier, (dom + 1, inner), is_relay)
    tell(barrier, (dom - 1, col), has_down, jnp.logical_not(replies_down))
    tell(barrier, (dom, inner), col > 0)
    tell(barrier, (dom, outer), has_outer, is_second)
    own_p = [
        pltpu.make_async_copy(p_hbm.at[:, y], near.at[pl.ds((y + 1) * ROWS + 2, 2)], own_sem.at[0])
        for y in range(rows_y)
    ]
    own_a = pltpu.make_async_copy(a_hbm, a_tiles, own_sem.at[1])
    for copy in own_p:
        copy.start()
    own_a.start()
    small = [
        pltpu.make_async_copy(source, target, small_sem.at[i])
        for i, (source, target) in enumerate(
            ((a_cols_hbm, a_cols), (slot_map_hbm, slot_map), (aggregate_hbm, aggregate))
        )
    ]
    for copy in small:
        copy.start()

    heard = (early_below, early_above, col != 1, has_outer & is_first, is_source)
    pl.semaphore_wait(barrier, sum(condition.astype(jnp.int32) for condition in heard))
    tell(ready.at[0], (dom + 1, col), replies_up, jnp.logical_not(is_corner))
    tell(ready.at[3], (dom - 1, col), replies_down)
    tell(ready.at[1], (dom, inner), col == 0)
    tell(ready.at[2], (dom, outer), has_outer, is_first)

    def arrive(semaphore, count):
        some = near.at[pl.ds(0, count)]
        pltpu.make_async_copy(some, some, semaphore).wait()

    def arrive_pieces(semaphore, count, *conditions):
        given(has_up & has_down, *conditions)(lambda: arrive(semaphore, 3 * count))
        given(has_up ^ has_down, *conditions)(lambda: arrive(semaphore, 2 * count))

    def along_dom(part, way):
        index = part * 2 + way
        return pltpu.make_async_remote_copy(
            src_ref=p_hbm.at[:, columns[part]],
            dst_ref=near.at[pl.ds((columns[part] + 1) * ROWS + 4 * way, 2)],
            send_sem=row_send.at[way],
            recv_sem=row_recv.at[index],
            device_id=(dom + 1 - 2 * way, col),
            device_id_type=MESH,
        )

    def along_col(part, piece):
        if piece == 1:
            source = p_hbm.at[:, columns[part]]
        else:
            source = near.at[pl.ds((columns[part] + 1) * ROWS + 2 * piece, 2)]
        target = (near, far_outer, near, far_inner)[part]
        return pltpu.make_async_remote_copy(
            src_ref=source,
            dst_ref=target.at[pl.ds(landing[part] * ROWS + 2 * piece, 2)],
            send_sem=col_send.at[part // 2],
            recv_sem=col_recv.at[part],
            device_id=(dom, (outer, outer, inner, inner)[part]),
            device_id_type=MESH,
        )

    def to_relay(part):
        return pltpu.make_async_remote_copy(
            src_ref=p_hbm.at[:, columns[part]],
            dst_ref=relayed.at[pl.ds(2 * part, 2)],
            send_sem=row_send.at[1],
            recv_sem=relay_recv,
            device_id=(dom - 1, inner),
            device_id_type=MESH,
        )

    def hand_on(part):
        theirs = (0, 1, 3, 2)[part]
        return pltpu.make_async_remote_copy(
            src_ref=relayed.at[pl.ds(2 * part, 2)],
            dst_ref=near.at[pl.ds((theirs + 1) * ROWS + 4, 2)],
            send_sem=relay_send,
            recv_sem=row_recv.at[2 * part + 1],
            device_id=(dom, inner),
            device_id_type=MESH,
        )

    by_row = [[along_dom(part, way) for way in range(2)] for part in range(4)]
    by_col = [[along_col(part, piece) for piece in range(3)] for part in range(4)]
    partners = (has_outer, has_outer, None, None)
    at_once = ((has_outer & is_first,) * 2) + ((col != 1,) * 2)
    for part in range(4):
        given(early_above)(by_row[part][0].start)
        given(early_below)(by_row[part][1].start)
        given(at_once[part])(by_col[part][1].start)

    @pl.when(is_source)
    def _():
        for part in range(4):
            to_relay(part).start()


    for copy in small:
        copy.wait()

    width_y = rows_y * n_col
    origin = (dom * rows_x - 2) * width_y + col * rows_y - 2
    inverse = -(-65536 // width_y)

    def tabulate(t):
        x, y = t // rows_y, lax.rem(t, rows_y)
        spots, groups = [], []
        for k in range(slots):
            where = a_cols[x, y, k]
            offset = where - origin
            near_x = (offset * inverse) >> 16
            near_y = offset - near_x * width_y
            spot = jnp.where((near_y == 0) | (near_y == 7), NEAR + near_x, (near_y - 1) * ROWS + near_x)
            spots.append(jnp.clip(spot, 0, NEAR + ROWS - 1))
            groups.append(jnp.where(where >= 0, slot_map[x, y, k], CSLOTS))
        count = jnp.int32(0)
        places = [jnp.int32(-1)] * slots
        ends[t * (CSLOTS + 1)] = 0
        for j in range(CSLOTS):
            for k in range(slots):
                member = groups[k] == j
                places[k] = jnp.where(member, count, places[k])
                count = count + member.astype(jnp.int32)
            ends[t * (CSLOTS + 1) + j + 1] = count
        for place in range(slots):
            slot, spot = jnp.int32(0), jnp.int32((y + 1) * ROWS + x + 2)
            for k in range(slots):
                chosen = places[k] == place
                slot = jnp.where(chosen, k, slot)
                spot = jnp.where(chosen, spots[k], spot)
            pick_a[t * slots + place] = t * slots + slot
            pick_g[t * slots + place] = spot

    def put_in_order(group):
        ts, first = members[group], sum(GROUPS[:group])
        sides = [lax.rem(aggregate[t // rows_y, lax.rem(t, rows_y)], n_col) - col + 1 for t in ts]
        count = jnp.int32(0)
        places = [jnp.int32(0)] * len(ts)
        side_ends[group * (SIDES + 1)] = 0
        for side in range(SIDES):
            for i in range(len(ts)):
                member = sides[i] == side
                places[i] = jnp.where(member, count, places[i])
                count = count + member.astype(jnp.int32)
            side_ends[group * (SIDES + 1) + side + 1] = count
        for place in range(len(ts)):
            chosen = jnp.int32(ts[0])
            for i, t in enumerate(ts):
                chosen = jnp.where(places[i] == place, t, chosen)
            order[first + place] = chosen

    def forward(part):
        for way in range(2):
            @given(gives[way])
            def _():
                by_row[part][way].wait_recv()
                given(partners[part])(by_col[part][2 * way].start)

    for t in members[0]:
        tabulate(t)

    @pl.when(late_below & jnp.logical_not(is_source))
    def _():
        pl.semaphore_wait(ready.at[0], 1)
        for part in range(4):
            by_row[part][1].start()

    @pl.when(late_above)
    def _():
        pl.semaphore_wait(ready.at[3], 1)
        for part in range(4):
            by_row[part][0].start()

    @pl.when(has_outer & is_second)
    def _():
        pl.semaphore_wait(ready.at[2], 1)
        for part in range(2):
            by_col[part][1].start()

    forward(0)
    for t in members[1] + members[2]:
        tabulate(t)
    forward(1)
    for group in range(3):
        put_in_order(group)
    arrive(own_sem.at[0], tiles)
    for t in range(tiles):
        turned = near[(1 + t % rows_y) * ROWS + 2 + t // rows_y].T
        p_turned[t] = jnp.concatenate([turned, turned], axis=1)
    own_a.wait()
    for i in range(8):
        sums[i][0] = jnp.zeros((tile, tile), F32)
    for group in range(3):
        totals[group][0] = jnp.zeros(totals[group].shape[1:], F32)

    @pl.when(col == 1)
    def _():
        pl.semaphore_wait(ready.at[1], 1)
        for part in (2, 3):
            by_col[part][1].start()

    @pl.when(is_relay)
    def _():
        arrive(relay_recv, tiles)
        for part in range(4):
            hand_on(part).start()

    forward(2)
    forward(3)
    for part in (0, 2):
        arrive_pieces(col_recv.at[part], 2, partners[part])

    ts = [order[i] for i in range(tiles)]

    def slot_sums(i, far):
        total = None
        for place in range(slots):
            at = ts[i] * slots + place
            spot = pick_g[at]
            if far is None:
                right = near[jnp.minimum(spot, NEAR - 1)]
            else:
                right = jnp.where(
                    spot >= NEAR, far[jnp.maximum(spot - NEAR, 0)], near[jnp.minimum(spot, NEAR - 1)]
                )
            term = dot(a_tiles[pick_a[at]], right)
            total = term if total is None else total + term
            sums[i][place + 1] = total

    def coarse_sums(i, group):
        place = i - sum(GROUPS[:group])
        t = ts[i]
        highs, lows = [], []
        for j in range(CSLOTS):
            base = t * (CSLOTS + 1) + j
            high, low = split(sums[i][ends[base + 1]] - sums[i][ends[base]])
            highs.append(high)
            lows.append(low)
        stacked = jnp.concatenate(
            [jnp.concatenate(highs, axis=1), jnp.concatenate(lows, axis=1)], axis=0
        )
        totals[group][place + 1] = totals[group][place] + dot(p_turned[t], stacked)

    group_of = [group for group, size in enumerate(GROUPS) for _ in range(size)]
    for i in range(tiles + 1):
        if i == GROUPS[0]:
            arrive_pieces(col_recv.at[1], 2, has_outer)
        if i == GROUPS[0] + GROUPS[1]:
            arrive_pieces(col_recv.at[3], 2)
        if i < tiles:
            slot_sums(i, (None, far_outer, far_inner)[group_of[i]])
        if i > 0:
            coarse_sums(i - 1, group_of[i - 1])

    def of_side(side, j):
        lanes = pl.ds(j * tile, tile)
        value = None
        for group in range(3):
            at = group * (SIDES + 1) + side
            part = totals[group][side_ends[at + 1], :, lanes] - totals[group][side_ends[at], :, lanes]
            value = part if value is None else value + part
        return value

    kept = pltpu.make_async_copy(away.at[0], arrived.at[0], own_sem.at[2])
    for partner in range(2):
        side = (2 * core, 2 - 2 * core)[partner]
        for j in range(CSLOTS):
            away[partner, j] = of_side(side, j).astype(BF16)
            copy = pltpu.make_async_remote_copy(
                src_ref=away.at[partner, j],
                dst_ref=arrived.at[partner, j],
                send_sem=away_send.at[partner],
                recv_sem=away_recv.at[partner],
                device_id=(dom, (outer, inner)[partner]),
                device_id_type=MESH,
            )
            given((has_outer, None)[partner])(copy.start)
    given(jnp.logical_not(has_outer))(kept.start)
    for j in range(CSLOTS):
        here[j] = of_side(1, j)

    for way in range(2):
        given(takes[way])(functools.partial(arrive, row_send.at[way], tiles))
    given(is_relay)(functools.partial(arrive, relay_send, tiles))
    arrive_pieces(col_send.at[0], 4, has_outer)
    arrive_pieces(col_send.at[1], 4)
    for partner in (1, 0):
        for semaphore in (away_send, away_recv):
            given((has_outer, None)[partner])(functools.partial(arrive, semaphore.at[partner], CSLOTS))
    given(jnp.logical_not(has_outer))(kept.wait)


def body(n_dom, n_col, a_tiles, p_tiles, a_cols, slot_map, aggregate):
    rows_x, rows_y, slots, tile, _ = a_tiles.shape
    tiles = rows_x * rows_y
    across = CSLOTS * tile
    any_space = pl.BlockSpec(memory_space=pl.ANY)
    operands = (a_cols, slot_map, aggregate, a_tiles.reshape(tiles * slots, tile, tile), p_tiles)
    here, arrived = pl.pallas_call(
        functools.partial(kernel, n_dom, n_col),
        out_shape=(
            pltpu.VMEM((CSLOTS, tile, tile), F32),
            pltpu.VMEM((2, CSLOTS, tile, tile), BF16),
        ),
        in_specs=[any_space] * 5,
        out_specs=(pl.BlockSpec(memory_space=pltpu.VMEM), any_space),
        scratch_shapes=[
            pltpu.VMEM((tiles * slots, tile, tile), BF16),
            pltpu.VMEM((NEAR, tile, tile), BF16),
            pltpu.VMEM((ROWS, tile, tile), BF16),
            pltpu.VMEM((ROWS, tile, tile), BF16),
            pltpu.VMEM((tiles, tile, tile), BF16),
            pltpu.VMEM((tiles, tile, 2 * tile), BF16),
        ]
        + [pltpu.VMEM((slots + 1, tile, tile), F32)] * tiles
        + [pltpu.VMEM((size + 1, tile, across), F32) for size in GROUPS]
        + [
            pltpu.SMEM(a_cols.shape, jnp.int32),
            pltpu.SMEM(slot_map.shape, jnp.int32),
            pltpu.SMEM(aggregate.shape, jnp.int32),
            pltpu.VMEM((2, CSLOTS, tile, tile), BF16),
            pltpu.SMEM((tiles * slots,), jnp.int32),
            pltpu.SMEM((tiles * slots,), jnp.int32),
            pltpu.SMEM((tiles * (CSLOTS + 1),), jnp.int32),
            pltpu.SMEM((tiles,), jnp.int32),
            pltpu.SMEM((3 * (SIDES + 1),), jnp.int32),
            pltpu.SemaphoreType.REGULAR((4,)),
            pltpu.SemaphoreType.DMA,
            pltpu.SemaphoreType.DMA,
            pltpu.SemaphoreType.DMA((3,)),
            pltpu.SemaphoreType.DMA((3,)),
            pltpu.SemaphoreType.DMA((2,)),
            pltpu.SemaphoreType.DMA((8,)),
            pltpu.SemaphoreType.DMA((2,)),
            pltpu.SemaphoreType.DMA((4,)),
            pltpu.SemaphoreType.DMA((2,)),
            pltpu.SemaphoreType.DMA((2,)),
        ],
        compiler_params=pltpu.CompilerParams(
            collective_id=0, has_side_effects=True, vmem_limit_bytes=24 * 2**20
        ),
    )(*(pltpu.with_memory_space_constraint(operand, pltpu.HBM) for operand in operands))
    result = here + arrived[0].astype(F32) + arrived[1].astype(F32)
    return result[None, None]


def solution(mesh):
    in_specs = (
        P("dom", "col", None, None, None),
        P("dom", "col", None, None),
        P("dom", "col", None),
        P("dom", "col", None),
        P("dom", "col"),
    )
    out_specs = P("dom", "col", None, None, None)
    call = functools.partial(body, mesh.shape["dom"], mesh.shape["col"])
    return jax.shard_map(call, mesh=mesh, in_specs=in_specs, out_specs=out_specs, check_vma=False)
```
